256 devices in a mesh: ctx: 8 (over y_lo, x), tp: 32 (over y_hi, z, core).
Axes of the slice: x: 4, y: 4 (y_hi: 2, y_lo: 2; y = y_hi * 2 + y_lo), z: 8, core: 2. Of those that a mesh axis runs over, the one named last changes fastest.
Arguments:
- hidden: bfloat16 [4096, 4096], P('ctx'), may hold values from -6 to 6
- mask_flags: int32 [4096], P('ctx'), may hold values 0 or 1
- mask_embed: bfloat16 [4096], replicated, may hold values from -6 to 6
- norm_gain: float32 [4096], replicated, may hold values from 0.1 to 1.9
- w_query: bfloat16 [4096, 4096], P(None, 'tp')
- w_key: bfloat16 [4096, 4096], P(None, 'tp')
- w_value: bfloat16 [4096, 4096], P(None, 'tp'), may hold values from -0.09375 to 0.09375
- w_out: bfloat16 [4096, 4096], P('tp'), may hold values from -0.5 to 0.5
Outputs:
- attended: bfloat16 [4096, 4096], P('ctx', 'tp')
The draws below stay inside these ranges and needn't reach their ends.
All inputs are finite; a program needn't handle non-finite values. No bound on the sum of `mask_flags` on one device may be relied on, other than what follows from the above.
Results may differ from the reference program's by a relative error of at most 0.017.
Values may be sent and summed in bfloat16 or wider, within the bound.
A program may use at most 64 MiB of HBM per device.

```python
import math
import jax
import jax.numpy as jnp
from jax import lax

D = 4096
HEADS = 32
HD = 128
SEQ = 4096
GROUP_HEADS = 1


def draw_hidden(key, part):
    key = jax.random.fold_in(key, 21)
    noise = jnp.clip(jax.random.normal(key, (SEQ, D), jnp.float32), -6.0, 6.0)
    result = noise
    return result.astype(jnp.bfloat16)


def draw_w_query(key, part):
    key = jax.random.fold_in(key, 11)
    result = jax.random.normal(key, (D, HEADS * HD), jnp.float32) / math.sqrt(D)
    return result.astype(jnp.bfloat16)


def draw_w_key(key, part):
    key = jax.random.fold_in(key, 12)
    result = jax.random.normal(key, (D, HEADS * HD), jnp.float32) / math.sqrt(D)
    return result.astype(jnp.bfloat16)


def with_ends(values, key, smallest, top_value):
    spot = [jax.random.randint(jax.random.fold_in(key, axis), (), 0, length) for axis, length in enumerate(values.shape)]
    widest = values.shape.index(max(values.shape))
    beside = spot[:widest] + [(spot[widest] + 1) % values.shape[widest]] + spot[widest + 1:]
    return values.at[tuple(spot)].set(smallest).at[tuple(beside)].set(top_value)


def block_levels(rng, shape, pieces, smallest, top_value):
    gain, own = 1.0, jax.random.fold_in(rng, 6)
    for axis_at, blocks in pieces:
        heights = jnp.exp(jax.random.uniform(jax.random.fold_in(own, axis_at), (blocks,), jnp.float32, smallest / len(pieces), top_value / len(pieces)))
        gain = gain * jnp.repeat(heights, shape[axis_at] // blocks).reshape([-1 if axis == axis_at else 1 for axis in range(len(shape))])
    return gain


def scatter_about(stream_key, dims, spread, bound, shards=(), dtype=jnp.bfloat16):
    array = jax.random.normal(stream_key, dims, jnp.float32) * spread
    if len(shards) > 0:
        array = block_levels(stream_key, dims, shards, -0.22, 0.18) * array
    return jnp.clip(array, min=-bound, max=bound).astype(dtype)


def setup_inputs(seed: int = 0) -> dict:
    seeds = jax.random.split(jax.random.key(seed), 9)
    return {
        "hidden": draw_hidden(jax.random.fold_in(seeds[8], 71), 0),
        "mask_flags": with_ends((jax.random.randint(seeds[1], (SEQ,), 0, 2) < 1).astype(jnp.int32), jax.random.fold_in(seeds[1], 1), 0, 1),
        "mask_embed": scatter_about(seeds[2], (D,), 1.0, 6.0),
        "norm_gain": jnp.clip(1.0 + 0.18 * jax.random.normal(seeds[3], (D,), jnp.float32), 0.1, 1.9),
        "w_query": draw_w_query(jax.random.fold_in(seeds[8], 71), 0),
        "w_key": draw_w_key(jax.random.fold_in(seeds[8], 71), 0),
        "w_value": scatter_about(seeds[6], (D, HEADS * HD), D ** -0.5, 0.09375, ((1, 32),)),
        "w_out": scatter_about(seeds[7], (HEADS * HD, D), HD ** -0.5, 0.5, ((0, 32),)),
    }


def rotate(block, angles):
    half = block.shape[-1] // 2
    first = block[..., :half]
    second = block[..., half:]
    cosine = jnp.cos(angles)[:, None, :]
    sine = jnp.sin(angles)[:, None, :]
    return jnp.concatenate([first * cosine - second * sine, second * cosine + first * sine], axis=-1)

def reference(hidden, mask_flags, mask_embed, norm_gain, w_query, w_key, w_value, w_out):
    tokens = jnp.where(mask_flags[:, None] == 1, mask_embed[None, :], hidden)
    floats = tokens.astype(jnp.float32)
    scale_rows = lax.rsqrt(lax.optimization_barrier(jnp.mean(floats * floats, axis=1, keepdims=True)) + 1e-05)
    normed = (floats * scale_rows * norm_gain[None, :]).astype(jnp.bfloat16)
    positions = jnp.arange(SEQ).astype(jnp.float32)
    freqs = jnp.power(500000.0, -2.0 * jnp.arange(HD // 2).astype(jnp.float32) / HD)
    angles = positions[:, None] * freqs[None, :]
    queries = jnp.dot(normed, w_query, preferred_element_type=jnp.float32).reshape(SEQ, HEADS, HD)
    keys = jnp.dot(normed, w_key, preferred_element_type=jnp.float32).reshape(SEQ, HEADS, HD)
    queries = rotate(queries, angles).astype(jnp.bfloat16)
    keys = rotate(keys, angles).astype(jnp.bfloat16)
    values = jnp.dot(normed, w_value, preferred_element_type=jnp.float32).astype(jnp.bfloat16).reshape(SEQ, HEADS, HD)

    def one_head(index):
        query_h = lax.dynamic_index_in_dim(queries, index, 1, False)
        key_h = lax.dynamic_index_in_dim(keys, index, 1, False)
        value_h = lax.dynamic_index_in_dim(values, index, 1, False)
        scores = jnp.dot(query_h, key_h.T, preferred_element_type=jnp.float32) / math.sqrt(HD)
        top = lax.optimization_barrier(jnp.max(scores, axis=1, keepdims=True))
        exps = jnp.exp(scores - top)
        total = lax.optimization_barrier(jnp.sum(exps, axis=1, keepdims=True))
        weights = exps.astype(jnp.bfloat16)
        return (jnp.dot(weights, value_h, preferred_element_type=jnp.float32) / total).astype(jnp.bfloat16)
    per_head = lax.map(one_head, jnp.arange(HEADS).astype(jnp.int32))
    mixed = jnp.transpose(per_head, (1, 0, 2)).reshape(SEQ, HEADS * HD)
    group_width = GROUP_HEADS * HD

    def add_group(running, index):
        start = index * group_width
        piece = lax.dynamic_slice_in_dim(mixed, start, group_width, 1)
        rows_part = lax.dynamic_slice_in_dim(w_out, start, group_width, 0)
        term = jnp.dot(piece, rows_part, preferred_element_type=jnp.float32).astype(jnp.bfloat16)
        term = lax.optimization_barrier(term)
        return (running + term.astype(jnp.float32), None)
    initial = jnp.zeros((SEQ, D), jnp.float32)
    summed, ignored = lax.scan(add_group, initial, jnp.arange(HEADS // GROUP_HEADS).astype(jnp.int32))
    return summed.astype(jnp.bfloat16)
```

```python
import math

import numpy as np
import jax
import jax.numpy as jnp
from jax import lax
from jax.sharding import PartitionSpec as P
from jax.experimental import pallas as pl
from jax.experimental.pallas import tpu as pltpu

D = 4096
HD = 128
SEQ = 4096
ROWS = 512
XROWS = 528
KB = 512
NKB = D // KB
R = 4
RB = ROWS // R
QB = 256
NZ = 8
NX = 4
MESH = pl.DeviceIdType.MESH
F32 = jnp.float32
BF16 = jnp.bfloat16


def rope_table():
    freqs = 500000.0 ** (-2.0 * np.arange(HD // 2) / HD)
    angles = np.arange(SEQ)[:, None] * freqs[None, :]
    return np.concatenate([np.cos(angles), np.sin(angles)], axis=1).astype(np.float32)


def kernel(hid, mask, emb, gain, wq, wk, wv, wo, tab, out,
           x, wkv_s, wq_s, emb_s, gain_s, mask_s, tab_s, maskc, ss, acc, qacc,
           kv, qs, m_s, o_s, mixed, mbuf, wd, part, rb, sb,
           ld_x, ld_k, ld_v, ld_s, ld_w, w_send, w_recv, sw_send, sw_recv,
           kv_send, kv_recv, m_send, m_recv, z_send, z_recv):
    ctx = lax.axis_index("ctx")
    tp = lax.axis_index("tp")
    xi, ylo = lax.rem(ctx, NX), lax.div(ctx, NX)
    yhi, z, core = lax.div(tp, 16), lax.rem(lax.div(tp, 2), NZ), lax.rem(tp, 2)
    diag = core == ylo
    off = core != ylo

    def dev(x_=xi, ylo_=ylo, yhi_=yhi, z_=z, core_=core):
        return (ylo_ * NX + x_, yhi_ * 16 + z_ * 2 + core_)

    xr, xl = lax.rem(xi + 1, NX), lax.rem(xi + NX - 1, NX)
    xo = lax.rem(xi + 2, NX)
    zr, zl = lax.rem(z + 1, NZ), lax.rem(z + NZ - 1, NZ)
    oc, oylo, oyhi = 1 - core, 1 - ylo, 1 - yhi

    loads = []
    c_gain = pltpu.make_async_copy(gain, gain_s, ld_s.at[0])
    c_emb = pltpu.make_async_copy(emb, emb_s, ld_s.at[1])
    c_mask = pltpu.make_async_copy(mask, mask_s, ld_s.at[2])
    c_tab = pltpu.make_async_copy(
        tab.at[pl.ds(pl.multiple_of(ctx * ROWS, ROWS), ROWS)], tab_s, ld_s.at[3])
    c_wq = pltpu.make_async_copy(wq, wq_s, ld_s.at[4])
    c_emb.start()
    c_gain.start()

    def xcopies(k):
        cols = pl.ds(pl.multiple_of(k * KB, KB), KB)
        return (
            pltpu.make_async_copy(hid.at[:, cols], x.at[pl.ds(0, ROWS), cols], ld_x.at[k]),
            pltpu.make_async_copy(wk.at[cols], wkv_s.at[cols, pl.ds(0, HD)], ld_k.at[k]),
            pltpu.make_async_copy(wv.at[cols], wkv_s.at[cols, pl.ds(HD, HD)], ld_v.at[k]),
        )

    def start_loads(k, _):
        for c in xcopies(k):
            c.start()
        return 0

    lax.fori_loop(0, NKB, start_loads, 0)
    c_mask.start()
    c_tab.start()
    c_wq.start()

    barrier = pltpu.get_barrier_semaphore()
    partners = [dev(x_=xr), dev(x_=xl), dev(z_=zr), dev(z_=zl), dev(core_=oc)]
    for c in (0, 1):
        partners += [dev(ylo_=oylo, core_=c), dev(yhi_=oyhi, core_=c),
                     dev(ylo_=oylo, yhi_=oyhi, core_=c)]
    for p in partners:
        pl.semaphore_signal(barrier, inc=1, device_id=p, device_id_type=MESH)
    pl.semaphore_wait(barrier, len(partners))

    my_rows = pl.ds(pl.multiple_of((yhi * 2 + core) * HD, HD), HD)

    def wsrc(half, zz, c):
        return wo.at[:, pl.ds(pl.multiple_of(half * 2048 + zz * 256 + c * HD, HD), HD)]

    def wdst(zz):
        return wd.at[my_rows, pl.ds(pl.multiple_of(zz * HD, HD), HD)]

    def wcopies(zz):
        return (
            pltpu.make_async_copy(wsrc(yhi, zz, core), wdst(zz), ld_w.at[0]),
            pltpu.make_async_remote_copy(
                wsrc(yhi, zz, oc), wdst(zz), w_send.at[0], w_recv.at[0],
                device_id=dev(core_=oc), device_id_type=MESH),
            pltpu.make_async_remote_copy(
                wsrc(oyhi, zz, 0), wdst(zz), w_send.at[1], w_recv.at[1 + core],
                device_id=dev(ylo_=oylo, yhi_=oyhi, core_=0), device_id_type=MESH),
            pltpu.make_async_remote_copy(
                wsrc(oyhi, zz, 1), wdst(zz), w_send.at[2], w_recv.at[1 + core],
                device_id=dev(ylo_=oylo, yhi_=oyhi, core_=1), device_id_type=MESH),
        )

    def start_w(zz, _):
        for c in wcopies(zz):
            c.start()
        return 0

    lax.fori_loop(0, NZ, start_w, 0)

    c_emb.wait()
    c_gain.wait()
    x[pl.ds(ROWS, XROWS - ROWS), :] = jnp.broadcast_to(emb_s[...], (XROWS - ROWS, D))
    ss[...] = jnp.zeros_like(ss)
    acc[...] = jnp.zeros_like(acc)

    def kstep(k, _):
        for c in xcopies(k):
            c.wait()
        cols = pl.ds(pl.multiple_of(k * KB, KB), KB)
        xf = x[:, cols].astype(F32)
        sq = xf * xf
        total = sq[:, :128]
        for j in range(1, KB // 128):
            total = total + sq[:, j * 128:(j + 1) * 128]
        ss[...] += total
        xg = (xf * gain_s[:, cols]).astype(BF16)
        x[:, cols] = xg
        acc[...] += jnp.dot(xg, wkv_s[cols, :], preferred_element_type=F32)
        return 0

    lax.fori_loop(0, NKB, kstep, 0)
    c_mask.wait()
    c_tab.wait()
    scale = lax.rsqrt(jnp.sum(ss[...], axis=1, keepdims=True) * (1.0 / D) + 1e-05)
    ss[...] = jnp.broadcast_to(scale, (XROWS, 128))
    flags = (mask_s[...] == 1).astype(F32)
    for i in range(ROWS // 128):
        maskc[pl.ds(i * 128, 128), :] = jnp.transpose(
            jnp.broadcast_to(flags[i:i + 1, :], (128, 128)))

    def chosen(ref, lo):
        u = ref[:, lo:lo + HD] * ss[...]
        return jnp.where(maskc[...] > 0.5, u[ROWS:ROWS + 1, :], u[:ROWS, :])

    lane = lax.broadcasted_iota(jnp.int32, (ROWS, HD), 1)

    def rope(u):
        t = tab_s[...]
        r = pltpu.roll(t, HD // 2, 1)
        c = jnp.where(lane < HD // 2, t, r)
        s = jnp.where(lane < HD // 2, -r, t)
        return u * c + pltpu.roll(u, HD // 2, 1) * s

    me = core * NX + xi
    put = jnp.where(diag, me, 8)
    kv[put, 0] = rope(chosen(acc, 0)).astype(BF16)
    kv[put, 1] = chosen(acc, HD).astype(BF16)

    partner = dev(ylo_=oylo, core_=oc)
    swap_k = pltpu.make_async_remote_copy(
        kv.at[8, 0], kv.at[ctx, 0], sw_send.at[0], sw_recv.at[0],
        device_id=partner, device_id_type=MESH)
    swap_v = pltpu.make_async_remote_copy(
        kv.at[8, 1], kv.at[ctx, 1], sw_send.at[1], sw_recv.at[1],
        device_id=partner, device_id_type=MESH)
    swap_q = pltpu.make_async_remote_copy(
        qs.at[1], qs.at[0], sw_send.at[2], sw_recv.at[2],
        device_id=partner, device_id_type=MESH)

    OWN, LEFT, RIGHT, OPP = 0, 1, 2, 3
    offs = (xi, xl, xr, xo)
    myset = jnp.where(diag, 0, 1)
    sends = {}
    n_send = [0]

    def kvcopy(pos_here, pos_there, which, to):
        slot = core * NX + offs[pos_here]
        c = pltpu.make_async_remote_copy(
            kv.at[slot, which], kv.at[slot, which], kv_send.at[n_send[0]],
            kv_recv.at[myset, pos_there, which], device_id=to, device_id_type=MESH)
        n_send[0] += 1
        return c

    to_r, to_l, to_c = dev(x_=xr), dev(x_=xl), dev(core_=oc)
    own_sends = [
        kvcopy(OWN, LEFT, 0, to_r), kvcopy(OWN, RIGHT, 1, to_l),
        kvcopy(OWN, LEFT, 1, to_r), kvcopy(OWN, RIGHT, 0, to_l),
        kvcopy(OWN, OWN, 0, to_c), kvcopy(OWN, OWN, 1, to_c),
    ]
    fwd_k = kvcopy(LEFT, OPP, 0, to_r)
    fwd_v = kvcopy(RIGHT, OPP, 1, to_l)
    core_sends = {(pos, w): kvcopy(pos, pos, w, to_c)
                  for pos in (LEFT, RIGHT, OPP) for w in (0, 1)}

    @pl.when(diag)
    def _():
        for c in own_sends:
            c.start()

    @pl.when(off)
    def _():
        swap_k.start()
        swap_v.start()

    c_wq.wait()
    qacc[...] = jnp.zeros_like(qacc)

    def qstep(k, _):
        cols = pl.ds(pl.multiple_of(k * KB, KB), KB)
        qacc[...] += jnp.dot(x[:, cols], wq_s[cols, :], preferred_element_type=F32)
        return 0

    lax.fori_loop(0, NKB, qstep, 0)
    q_factor = math.log2(math.e) / math.sqrt(HD)
    qs[jnp.where(diag, 0, 1)] = (rope(chosen(qacc, 0)) * q_factor).astype(BF16)

    @pl.when(off)
    def _():
        swap_q.start()
        swap_k.wait_recv()
        swap_v.wait_recv()
        for c in own_sends:
            c.start()
        swap_q.wait_recv()

    def arrived(st, pos, which):
        slot = (ylo if st == 0 else oylo) * NX + offs[pos]
        pltpu.make_async_copy(kv.at[slot, which], kv.at[slot, which],
                              kv_recv.at[st, pos, which]).wait()

    ones = jnp.ones((ROWS, HD), BF16)

    def attend_rows(slot, i, first):
        rows = pl.ds(i * QB, QB)
        s = lax.dot_general(qs[0, rows, :], kv[slot, 0], (((1,), (1,)), ((), ())),
                            preferred_element_type=F32)
        top = jnp.broadcast_to(jnp.max(s, axis=1, keepdims=True), (QB, HD))
        if not first:
            old = m_s[rows, :]
            top = jnp.maximum(top, old)
        m_s[rows, :] = top
        p = jnp.exp2(s - jnp.concatenate([top] * (ROWS // HD), axis=1)).astype(BF16)
        v = jnp.concatenate([kv[slot, 1], ones], axis=1)
        add = jnp.dot(p, v, preferred_element_type=F32)
        if first:
            o_s[rows, :] = add
        else:
            alpha = jnp.exp2(old - top)
            o_s[rows, :] = o_s[rows, :] * jnp.concatenate([alpha, alpha], axis=1) + add

    def attend(st, pos):
        slot = (ylo if st == 0 else oylo) * NX + offs[pos]
        for i in range(ROWS // QB):
            attend_rows(slot, i, st == 0 and pos == OWN)

    for st, mine, other in ((0, diag, off), (1, off, diag)):
        @pl.when(other)
        def _():
            arrived(st, OWN, 0)
            arrived(st, OWN, 1)

        attend(st, OWN)

        for pos, which, fwd in ((LEFT, 0, fwd_k), (RIGHT, 1, fwd_v), (LEFT, 1, None), (RIGHT, 0, None)):
            arrived(st, pos, which)

            @pl.when(mine)
            def _():
                if fwd is not None:
                    fwd.start()
                core_sends[pos, which].start()

        attend(st, LEFT)
        attend(st, RIGHT)
        for which in (0, 1):
            arrived(st, OPP, which)

            @pl.when(mine)
            def _():
                core_sends[OPP, which].start()

        attend(st, OPP)

    hslot = yhi * 2 + ylo
    mcols = pl.ds(pl.multiple_of(hslot * HD, HD), HD)
    dests = [dev(ylo_=core, yhi_=h, core_=c) for h in (yhi, oyhi) for c in (core, oc)]

    def mcopy(r, j):
        rows = pl.ds(r * RB, RB)
        return pltpu.make_async_remote_copy(
            mixed.at[rows], mbuf.at[rows, mcols], m_send.at[j, r], m_recv.at[hslot, r],
            device_id=dests[j], device_id_type=MESH)

    for r in range(R):
        rows = pl.ds(r * RB, RB)
        o = o_s[rows, :]
        mix = (o[:, :HD] / o[:, HD:]).astype(BF16)
        mixed[rows, :] = mix

        @pl.when(off)
        def _():
            mcopy(r, 0).start()

        @pl.when(diag)
        def _():
            mbuf[rows, mcols] = mix

        for j in (1, 2, 3):
            mcopy(r, j).start()

    own_w = wd.at[my_rows]
    pltpu.make_async_copy(own_w, own_w, ld_w.at[0]).wait()
    for n, slot in ((0, yhi * 2 + oc), (1, oyhi * 2), (2, oyhi * 2 + 1)):
        ref = wd.at[pl.ds(pl.multiple_of(slot * HD, HD), HD)]
        pltpu.make_async_copy(ref, ref, w_recv.at[n]).wait()

    def hops(d, r):
        return NZ // 2 if (d == 0) == (r < R // 2) else NZ // 2 - 1

    def zcopy(d, r, i):
        return pltpu.make_async_remote_copy(
            sb.at[d, r, i], rb.at[d, r, i], z_send.at[d, r, i], z_recv.at[d, r, i],
            device_id=dev(z_=zr if d == 0 else zl), device_id_type=MESH)

    def piece(r, dest):
        return part[pl.ds(r * RB, RB), pl.ds(pl.multiple_of(dest * HD, HD), HD)]

    def partial(r):
        rows = pl.ds(r * RB, RB)
        for h in range(4):
            def wait_slot():
                ref = mbuf.at[rows, pl.ds(h * HD, HD)]
                pltpu.make_async_copy(ref, ref, m_recv.at[h, r]).wait()

            pl.when(jnp.logical_or(off, hslot != h))(wait_slot)
        part[rows, :] = jnp.dot(mbuf[rows, :], wd[...], preferred_element_type=F32)

    steps = NZ // 2
    for w in range(R + steps):
        if w < R:
            partial(w)
        for r in range(R):
            i = w - r
            if i < 0 or i > steps:
                continue
            for d in (0, 1):
                n = hops(d, r)
                if i >= n:
                    continue
                sign = 1 if d == 0 else -1
                dest = lax.rem(z + NZ + sign * (n - i), NZ)
                val = piece(r, dest)
                if i > 0:
                    zcopy(d, r, i - 1).wait_recv()
                    val = val + rb[d, r, i - 1].astype(F32)
                sb[d, r, i] = val.astype(BF16)
                zcopy(d, r, i).start()
            if i == steps:
                val = piece(r, z)
                for d in (0, 1):
                    last = hops(d, r) - 1
                    zcopy(d, r, last).wait_recv()
                    val = val + rb[d, r, last].astype(F32)
                out[pl.ds(r * RB, RB), :] = val.astype(BF16)

    for n, c in ((0, oc), (1, 0), (2, 1)):
        pltpu.make_async_copy(own_w, own_w, w_send.at[n]).wait()

    @pl.when(off)
    def _():
        for c in (swap_k, swap_v, swap_q):
            c.wait_send()

    for c in own_sends + [fwd_k, fwd_v] + list(core_sends.values()):
        c.wait_send()
    for r in range(R):
        @pl.when(off)
        def _():
            mcopy(r, 0).wait_send()

        for j in (1, 2, 3):
            mcopy(r, j).wait_send()
        for d in (0, 1):
            for i in range(hops(d, r)):
                zcopy(d, r, i).wait_send()


def on_device(hidden, mask_flags, mask_embed, norm_gain, w_query, w_key, w_value, w_out):
    any_spec = pl.BlockSpec(memory_space=pl.ANY)
    dma = pltpu.SemaphoreType.DMA
    return pl.pallas_call(
        kernel,
        out_shape=jax.ShapeDtypeStruct((ROWS, HD), BF16),
        in_specs=[any_spec] * 9,
        out_specs=pl.BlockSpec(memory_space=pltpu.VMEM),
        scratch_shapes=[
            pltpu.VMEM((XROWS, D), BF16),
            pltpu.VMEM((D, 2 * HD), BF16),
            pltpu.VMEM((D, HD), BF16),
            pltpu.VMEM((1, D), BF16),
            pltpu.VMEM((1, D), F32),
            pltpu.VMEM((ROWS // 128, 128), jnp.int32),
            pltpu.VMEM((ROWS, HD), F32),
            pltpu.VMEM((ROWS, 128), F32),
            pltpu.VMEM((XROWS, 128), F32),
            pltpu.VMEM((XROWS, 2 * HD), F32),
            pltpu.VMEM((XROWS, HD), F32),
            pltpu.VMEM((9, 2, ROWS, HD), BF16),
            pltpu.VMEM((2, ROWS, HD), BF16),
            pltpu.VMEM((ROWS, HD), F32),
            pltpu.VMEM((ROWS, 2 * HD), F32),
            pltpu.VMEM((ROWS, HD), BF16),
            pltpu.VMEM((ROWS, 4 * HD), BF16),
            pltpu.VMEM((4 * HD, NZ * HD), BF16),
            pltpu.VMEM((ROWS, NZ * HD), F32),
            pltpu.VMEM((2, R, NZ // 2, RB, HD), BF16),
            pltpu.VMEM((2, R, NZ // 2, RB, HD), BF16),
            dma((NKB,)), dma((NKB,)), dma((NKB,)), dma((5,)), dma((1,)),
            dma((3,)), dma((3,)), dma((3,)), dma((3,)),
            dma((14,)), dma((2, 4, 2)), dma((4, R)), dma((4, R)),
            dma((2, R, NZ // 2)), dma((2, R, NZ // 2)),
        ],
        compiler_params=pltpu.CompilerParams(
            collective_id=0, has_side_effects=True, vmem_limit_bytes=48 * 1024 * 1024),
    )(hidden, mask_flags.reshape(ROWS // 128, 128), mask_embed.reshape(1, D),
      norm_gain.reshape(1, D), w_query, w_key, w_value, w_out, jnp.asarray(rope_table()))


def solution(mesh):
    in_specs = (
        P("ctx", None),
        P("ctx"),
        P(),
        P(),
        P(None, "tp"),
        P(None, "tp"),
        P(None, "tp"),
        P("tp", None),
    )
    return jax.shard_map(
        on_device, mesh=mesh, in_specs=in_specs, out_specs=P("ctx", "tp"), check_vma=False
    )
```

```python
import math

import numpy as np
import jax
import jax.numpy as jnp
from jax import lax
from jax.sharding import PartitionSpec as P
from jax.experimental import pallas as pl
from jax.experimental.pallas import tpu as pltpu

D = 4096
HD = 128
SEQ = 4096
ROWS = 512
XROWS = 528
KB = 512
NKB = D // KB
R = 4
RB = ROWS // R
QB = 256
NZ = 8
NX = 4
MESH = pl.DeviceIdType.MESH
F32 = jnp.float32
BF16 = jnp.bfloat16


def rope_table():
    freqs = 500000.0 ** (-2.0 * np.arange(HD // 2) / HD)
    angles = np.arange(SEQ)[:, None] * freqs[None, :]
    return np.concatenate([np.cos(angles), np.sin(angles)], axis=1).astype(np.float32)


def kernel(hid, mask, emb, gain, wq, wk, wv, wo, tab, out,
           x, wkv_s, wq_s, emb_s, gain_s, mask_s, tab_s, maskc, ss, acc, qacc,
           kv, qs, m_s, o_s, mixed, mbuf, wd, part, rb, sb,
           ld_x, ld_k, ld_v, ld_s, ld_w, w_send, w_recv, sw_send, sw_recv,
           kv_send, kv_recv, m_send, m_recv, p_send, z_send, z_recv):
    ctx = lax.axis_index("ctx")
    tp = lax.axis_index("tp")
    xi, ylo = lax.rem(ctx, NX), lax.div(ctx, NX)
    yhi, z, core = lax.div(tp, 16), lax.rem(lax.div(tp, 2), NZ), lax.rem(tp, 2)
    diag = core == ylo
    off = core != ylo

    def dev(x_=xi, ylo_=ylo, yhi_=yhi, z_=z, core_=core):
        return (ylo_ * NX + x_, yhi_ * 16 + z_ * 2 + core_)

    xr, xl = lax.rem(xi + 1, NX), lax.rem(xi + NX - 1, NX)
    xo = lax.rem(xi + 2, NX)
    zr, zl = lax.rem(z + 1, NZ), lax.rem(z + NZ - 1, NZ)
    oc, oylo, oyhi = 1 - core, 1 - ylo, 1 - yhi

    c_gain = pltpu.make_async_copy(gain, gain_s, ld_s.at[0])
    c_emb = pltpu.make_async_copy(emb, emb_s, ld_s.at[1])
    c_mask = pltpu.make_async_copy(mask, mask_s, ld_s.at[2])
    c_tab = pltpu.make_async_copy(
        tab.at[pl.ds(pl.multiple_of(ctx * ROWS, ROWS), ROWS)], tab_s, ld_s.at[3])
    c_wq = pltpu.make_async_copy(wq, wq_s, ld_s.at[4])
    c_emb.start()
    c_gain.start()

    def xcopies(k):
        cols = pl.ds(pl.multiple_of(k * KB, KB), KB)
        return (
            pltpu.make_async_copy(hid.at[:, cols], x.at[pl.ds(0, ROWS), cols], ld_x.at[k]),
            pltpu.make_async_copy(wk.at[cols], wkv_s.at[cols, pl.ds(0, HD)], ld_k.at[k]),
            pltpu.make_async_copy(wv.at[cols], wkv_s.at[cols, pl.ds(HD, HD)], ld_v.at[k]),
        )

    def start_loads(k, _):
        for c in xcopies(k):
            c.start()
        return 0

    lax.fori_loop(0, NKB, start_loads, 0)
    c_mask.start()
    c_tab.start()
    c_wq.start()

    barrier = pltpu.get_barrier_semaphore()
    partners = [dev(x_=xr), dev(x_=xl), dev(x_=xo), dev(z_=zr), dev(z_=zl), dev(core_=oc)]
    for c in (0, 1):
        partners += [dev(ylo_=oylo, core_=c), dev(yhi_=oyhi, core_=c),
                     dev(ylo_=oylo, yhi_=oyhi, core_=c)]
    for p in partners:
        pl.semaphore_signal(barrier, inc=1, device_id=p, device_id_type=MESH)

    my_rows = pl.ds(pl.multiple_of((yhi * 2 + core) * HD, HD), HD)

    def wsrc(half, zz, c):
        return wo.at[:, pl.ds(pl.multiple_of(half * 2048 + zz * 256 + c * HD, HD), HD)]

    def wdst(zz):
        return wd.at[my_rows, pl.ds(pl.multiple_of(zz * HD, HD), HD)]

    def wcopies(zz):
        return (
            pltpu.make_async_copy(wsrc(yhi, zz, core), wdst(zz), ld_w.at[0]),
            pltpu.make_async_remote_copy(
                wsrc(yhi, zz, oc), wdst(zz), w_send.at[0], w_recv.at[0],
                device_id=dev(core_=oc), device_id_type=MESH),
            pltpu.make_async_remote_copy(
                wsrc(oyhi, zz, 0), wdst(zz), w_send.at[1], w_recv.at[1 + core],
                device_id=dev(ylo_=oylo, yhi_=oyhi, core_=0), device_id_type=MESH),
            pltpu.make_async_remote_copy(
                wsrc(oyhi, zz, 1), wdst(zz), w_send.at[2], w_recv.at[1 + core],
                device_id=dev(ylo_=oylo, yhi_=oyhi, core_=1), device_id_type=MESH),
        )

    def start_w(zz, _):
        for c in wcopies(zz):
            c.start()
        return 0

    c_emb.wait()
    c_gain.wait()
    x[pl.ds(ROWS, XROWS - ROWS), :] = jnp.broadcast_to(emb_s[...].reshape(1, D), (XROWS - ROWS, D))
    ss[...] = jnp.zeros_like(ss)
    acc[...] = jnp.zeros_like(acc)

    def kstep(k, _):
        for c in xcopies(k):
            c.wait()
        cols = pl.ds(pl.multiple_of(k * KB, KB), KB)
        xf = x[:, cols].astype(F32)
        sq = xf * xf
        total = sq[:, :128]
        for j in range(1, KB // 128):
            total = total + sq[:, j * 128:(j + 1) * 128]
        ss[...] += total
        xg = (xf * gain_s[:, cols]).astype(BF16)
        x[:, cols] = xg
        acc[...] += jnp.dot(xg, wkv_s[cols, :], preferred_element_type=F32)
        return 0

    lax.fori_loop(0, NKB, kstep, 0)
    c_mask.wait()
    c_tab.wait()
    scale = lax.rsqrt(jnp.sum(ss[...], axis=1, keepdims=True) * (1.0 / D) + 1e-05)
    ss[...] = jnp.broadcast_to(scale, (XROWS, 128))
    flags = (mask_s[...] == 1).astype(F32)
    for i in range(ROWS // 128):
        maskc[pl.ds(i * 128, 128), :] = jnp.transpose(
            jnp.broadcast_to(flags[i:i + 1, :], (128, 128)))

    def chosen(ref, lo):
        u = ref[:, lo:lo + HD] * ss[...]
        return jnp.where(maskc[...] > 0.5, u[ROWS:ROWS + 1, :], u[:ROWS, :])

    lane = lax.broadcasted_iota(jnp.int32, (ROWS, HD), 1)

    def rope(u):
        t = tab_s[...]
        r = pltpu.roll(t, HD // 2, 1)
        c = jnp.where(lane < HD // 2, t, r)
        s = jnp.where(lane < HD // 2, -r, t)
        return u * c + pltpu.roll(u, HD // 2, 1) * s

    me = core * NX + xi
    put = jnp.where(diag, me, 8)
    kv[put, 0] = rope(chosen(acc, 0)).astype(BF16)
    kv[put, 1] = chosen(acc, HD).astype(BF16)

    pl.semaphore_wait(barrier, len(partners))

    partner = dev(ylo_=oylo, core_=oc)
    swap_k = pltpu.make_async_remote_copy(
        kv.at[8, 0], kv.at[ctx, 0], sw_send.at[0], sw_recv.at[0],
        device_id=partner, device_id_type=MESH)
    swap_v = pltpu.make_async_remote_copy(
        kv.at[8, 1], kv.at[ctx, 1], sw_send.at[1], sw_recv.at[1],
        device_id=partner, device_id_type=MESH)
    swap_q = pltpu.make_async_remote_copy(
        qs.at[1], qs.at[0], sw_send.at[2], sw_recv.at[2],
        device_id=partner, device_id_type=MESH)

    OWN, LEFT, RIGHT, OPP = 0, 1, 2, 3
    offs = (xi, xl, xr, xo)
    myset = jnp.where(diag, 0, 1)
    n_send = [0]

    def kvcopy(pos_here, pos_there, which, to, n=None):
        slot = core * NX + offs[pos_here]
        c = pltpu.make_async_remote_copy(
            kv.at[slot, which], kv.at[slot, which], kv_send.at[n_send[0] if n is None else n],
            kv_recv.at[myset, pos_there, which], device_id=to, device_id_type=MESH)
        n_send[0] += n is None
        return c

    to_r, to_l, to_c = dev(x_=xr), dev(x_=xl), dev(core_=oc)
    own_sends = [
        kvcopy(OWN, LEFT, 0, to_r), kvcopy(OWN, RIGHT, 1, to_l),
        kvcopy(OWN, LEFT, 1, to_r), kvcopy(OWN, RIGHT, 0, to_l),
        kvcopy(OWN, OWN, 0, to_c), kvcopy(OWN, OWN, 1, to_c),
    ]
    fwd_k = kvcopy(LEFT, OPP, 0, to_r)
    fwd_v = kvcopy(RIGHT, OPP, 1, to_l)
    to_o = dev(x_=xo)
    far_sends = [kvcopy(OWN, OPP, w, to_o, n_send[0] - 2 + w) for w in (0, 1)]
    core_sends = {(pos, w): kvcopy(pos, pos, w, to_c)
                  for pos in (LEFT, RIGHT, OPP) for w in (0, 1)}

    @pl.when(diag)
    def _():
        for c in own_sends:
            c.start()

    @pl.when(off)
    def _():
        swap_k.start()
        swap_v.start()

    lax.fori_loop(0, NZ, start_w, 0)

    c_wq.wait()
    qacc[...] = jnp.zeros_like(qacc)

    def qstep(k, _):
        cols = pl.ds(pl.multiple_of(k * KB, KB), KB)
        qacc[...] += jnp.dot(x[:, cols], wq_s[cols, :], preferred_element_type=F32)
        return 0

    lax.fori_loop(0, NKB, qstep, 0)
    q_factor = math.log2(math.e) / math.sqrt(HD)
    qs[jnp.where(diag, 0, 1)] = (rope(chosen(qacc, 0)) * q_factor).astype(BF16)

    @pl.when(off)
    def _():
        swap_q.start()
        swap_k.wait_recv()
        swap_v.wait_recv()
        for c in far_sends + own_sends:
            c.start()
        swap_q.wait_recv()

    def arrived(st, pos, which):
        slot = (ylo if st == 0 else oylo) * NX + offs[pos]
        pltpu.make_async_copy(kv.at[slot, which], kv.at[slot, which],
                              kv_recv.at[st, pos, which]).wait()

    ones = jnp.ones((ROWS, HD), BF16)

    def attend_rows(slot, i, first):
        rows = pl.ds(i * QB, QB)
        s = lax.dot_general(qs[0, rows, :], kv[slot, 0], (((1,), (1,)), ((), ())),
                            preferred_element_type=F32)
        top = jnp.broadcast_to(jnp.max(s, axis=1, keepdims=True), (QB, HD))
        if not first:
            old = m_s[rows, :]
            top = jnp.maximum(top, old)
        m_s[rows, :] = top
        p = jnp.exp2(s - jnp.concatenate([top] * (ROWS // HD), axis=1)).astype(BF16)
        v = jnp.concatenate([kv[slot, 1], ones], axis=1)
        add = jnp.dot(p, v, preferred_element_type=F32)
        if first:
            o_s[rows, :] = add
        else:
            alpha = jnp.exp2(old - top)
            o_s[rows, :] = o_s[rows, :] * jnp.concatenate([alpha, alpha], axis=1) + add

    def attend(st, pos):
        slot = (ylo if st == 0 else oylo) * NX + offs[pos]
        for i in range(ROWS // QB):
            attend_rows(slot, i, st == 0 and pos == OWN)

    for st, mine, other in ((0, diag, off), (1, off, diag)):
        @pl.when(other)
        def _():
            arrived(st, OWN, 0)
            arrived(st, OWN, 1)

        attend(st, OWN)

        for pos, which, fwd in ((LEFT, 0, fwd_k), (RIGHT, 1, fwd_v), (LEFT, 1, None), (RIGHT, 0, None)):
            arrived(st, pos, which)

            @pl.when(mine)
            def _():
                if fwd is not None and st == 0:
                    fwd.start()
                core_sends[pos, which].start()

        attend(st, LEFT)
        attend(st, RIGHT)
        for which in (0, 1):
            arrived(st, OPP, which)

            @pl.when(mine)
            def _():
                core_sends[OPP, which].start()

        if st == 0:
            attend(st, OPP)

    hslot = yhi * 2 + ylo
    mcols = pl.ds(pl.multiple_of(hslot * HD, HD), HD)

    def mcopy(r, j):
        rows = pl.ds(r * RB, RB)
        to = (dev(ylo_=core, yhi_=yhi, core_=r % 2), dev(ylo_=core, yhi_=oyhi, core_=r % 2), to_c)[j]
        return pltpu.make_async_remote_copy(
            mixed.at[rows], mbuf.at[rows, mcols], m_send.at[j % 2, r], m_recv.at[hslot, r],
            device_id=to, device_id_type=MESH)

    last = oylo * NX + xo
    for i in range(ROWS // QB):
        attend_rows(last, i, False)
        for r in range(i * R * QB // ROWS, (i + 1) * R * QB // ROWS):
            rows = pl.ds(r * RB, RB)
            o = o_s[rows, :]
            mix = (o[:, :HD] / o[:, HD:]).astype(BF16)
            mixed[rows, :] = mix

            @pl.when(off)
            def _():
                mcopy(r, 0).start()

            @pl.when(diag)
            def _():
                mbuf[rows, mcols] = mix
                mcopy(r, 2).start()

            mcopy(r, 1).start()

    own_w = wd.at[my_rows]
    pltpu.make_async_copy(own_w, own_w, ld_w.at[0]).wait()
    for n, slot in ((0, yhi * 2 + oc), (1, oyhi * 2), (2, oyhi * 2 + 1)):
        ref = wd.at[pl.ds(pl.multiple_of(slot * HD, HD), HD)]
        pltpu.make_async_copy(ref, ref, w_recv.at[n]).wait()

    def hops(d, r):
        return NZ // 2 if (d == 0) == (r < R // 2) else NZ // 2 - 1

    def zcopy(d, r, i):
        return pltpu.make_async_remote_copy(
            sb.at[d, r, i], rb.at[d, r, i], z_send.at[d, r, i], z_recv.at[d, r, i],
            device_id=dev(z_=zr if d == 0 else zl), device_id_type=MESH)

    def piece(r, dest):
        return part[pl.ds(r * RB, RB), pl.ds(pl.multiple_of(dest * HD, HD), HD)]

    def mpass(h, r):
        ref = mbuf.at[pl.ds(r * RB, RB), pl.ds(h * HD, HD)]
        return pltpu.make_async_remote_copy(
            ref, ref, p_send.at[h, r], m_recv.at[h, r], device_id=to_c, device_id_type=MESH)

    def partial(r):
        rows = pl.ds(r * RB, RB)
        for h in range(4):
            def wait_slot():
                ref = mbuf.at[rows, pl.ds(h * HD, HD)]
                pltpu.make_async_copy(ref, ref, m_recv.at[h, r]).wait()

            def pass_on():
                mpass(h, r).start()

            pl.when(jnp.logical_or(off, hslot != h))(wait_slot)
            pl.when(jnp.logical_and(core == r % 2, hslot != h))(pass_on)
        part[rows, :] = jnp.dot(mbuf[rows, :], wd[...], preferred_element_type=F32)

    steps = NZ // 2

    def zstep(r, i):
        for d in (0, 1):
            n = hops(d, r)
            if i >= n:
                continue
            sign = 1 if d == 0 else -1
            dest = lax.rem(z + NZ + sign * (n - i), NZ)
            val = piece(r, dest)
            if i > 0:
                zcopy(d, r, i - 1).wait_recv()
                val = val + rb[d, r, i - 1].astype(F32)
            sb[d, r, i] = val.astype(BF16)
            zcopy(d, r, i).start()
        if i == steps:
            val = piece(r, z)
            for d in (0, 1):
                end = hops(d, r) - 1
                zcopy(d, r, end).wait_recv()
                val = val + rb[d, r, end].astype(F32)
            out[pl.ds(r * RB, RB), :] = val.astype(BF16)

    for r in range(R):
        partial(r)
        zstep(r, 0)
    for i in range(1, steps + 1):
        for r in range(R):
            zstep(r, i)
    for n, c in ((0, oc), (1, 0), (2, 1)):
        pltpu.make_async_copy(own_w, own_w, w_send.at[n]).wait()

    @pl.when(off)
    def _():
        for c in (swap_k, swap_v, swap_q):
            c.wait_send()

    for c in own_sends + [fwd_k, fwd_v] + list(core_sends.values()):
        c.wait_send()
    for r in range(R):
        mcopy(r, 0).wait_send()
        mcopy(r, 1).wait_send()
        for h in range(4):
            pl.when(jnp.logical_and(core == r % 2, hslot != h))(mpass(h, r).wait_send)
        for d in (0, 1):
            for i in range(hops(d, r)):
                zcopy(d, r, i).wait_send()


def on_device(hidden, mask_flags, mask_embed, norm_gain, w_query, w_key, w_value, w_out):
    any_spec = pl.BlockSpec(memory_space=pl.ANY)
    dma = pltpu.SemaphoreType.DMA
    return pl.pallas_call(
        kernel,
        out_shape=jax.ShapeDtypeStruct((ROWS, HD), BF16),
        in_specs=[any_spec] * 9,
        out_specs=pl.BlockSpec(memory_space=pltpu.VMEM),
        scratch_shapes=[
            pltpu.VMEM((XROWS, D), BF16),
            pltpu.VMEM((D, 2 * HD), BF16),
            pltpu.VMEM((D, HD), BF16),
            pltpu.VMEM((D,), BF16),
            pltpu.VMEM((1, D), F32),
            pltpu.VMEM((ROWS // 128, 128), jnp.int32),
            pltpu.VMEM((ROWS, HD), F32),
            pltpu.VMEM((ROWS, 128), F32),
            pltpu.VMEM((XROWS, 128), F32),
            pltpu.VMEM((XROWS, 2 * HD), F32),
            pltpu.VMEM((XROWS, HD), F32),
            pltpu.VMEM((9, 2, ROWS, HD), BF16),
            pltpu.VMEM((2, ROWS, HD), BF16),
            pltpu.VMEM((ROWS, HD), F32),
            pltpu.VMEM((ROWS, 2 * HD), F32),
            pltpu.VMEM((ROWS, HD), BF16),
            pltpu.VMEM((ROWS, 4 * HD), BF16),
            pltpu.VMEM((4 * HD, NZ * HD), BF16),
            pltpu.VMEM((ROWS, NZ * HD), F32),
            pltpu.VMEM((2, R, NZ // 2, RB, HD), BF16),
            pltpu.VMEM((2, R, NZ // 2, RB, HD), BF16),
            dma((NKB,)), dma((NKB,)), dma((NKB,)), dma((5,)), dma((1,)),
            dma((3,)), dma((3,)), dma((3,)), dma((3,)),
            dma((14,)), dma((2, 4, 2)), dma((2, R)), dma((4, R)), dma((4, R)),
            dma((2, R, NZ // 2)), dma((2, R, NZ // 2)),
        ],
        compiler_params=pltpu.CompilerParams(
            collective_id=0, has_side_effects=True, vmem_limit_bytes=62 * 1024 * 1024),
    )(hidden, mask_flags.reshape(ROWS // 128, 128), mask_embed,
      norm_gain.reshape(1, D), w_query, w_key, w_value, w_out, jnp.asarray(rope_table()))


def solution(mesh):
    in_specs = (
        P("ctx", None),
        P("ctx"),
        P(),
        P(),
        P(None, "tp"),
        P(None, "tp"),
        P(None, "tp"),
        P("tp", None),
    )
    return jax.shard_map(
        on_device, mesh=mesh, in_specs=in_specs, out_specs=P("ctx", "tp"), check_vma=False
    )
```

```python
import math

import numpy as np
import jax
import jax.numpy as jnp
from jax import lax
from jax.sharding import PartitionSpec as P
from jax.experimental import pallas as pl
from jax.experimental.pallas import tpu as pltpu

D = 4096
HD = 128
SEQ = 4096
ROWS = 512
XROWS = 528
KB = 1024
NKB = D // KB
KQ = 512
R = 4
RB = ROWS // R
QB = 256
NZ = 8
NX = 4
MESH = pl.DeviceIdType.MESH
F32 = jnp.float32
BF16 = jnp.bfloat16


def rope_table():
    freqs = 500000.0 ** (-2.0 * np.arange(HD // 2) / HD)
    angles = np.arange(SEQ)[:, None] * freqs[None, :]
    return np.concatenate([np.cos(angles), np.sin(angles)], axis=1).astype(np.float32)


def kernel(hid, mask, emb, gain, wq, wk, wv, wo, tab, out,
           x, wkv_s, wq_s, emb_s, gain_s, mask_s, tab_s, maskc, ss, acc, qacc,
           kv, qs, m_s, o_s, mixed, mbuf, wd, part, rb, sb,
           ld_x, ld_k, ld_v, ld_s, ld_w, w_send, w_recv, sw_send, sw_recv,
           kv_send, kv_recv, opp_recv, m_send, m_recv, p_send, z_send, z_recv):
    ctx = lax.axis_index("ctx")
    tp = lax.axis_index("tp")
    xi, ylo = lax.rem(ctx, NX), lax.div(ctx, NX)
    yhi, z, core = lax.div(tp, 16), lax.rem(lax.div(tp, 2), NZ), lax.rem(tp, 2)
    diag = core == ylo
    off = core != ylo

    def dev(x_=xi, ylo_=ylo, yhi_=yhi, z_=z, core_=core):
        return (ylo_ * NX + x_, yhi_ * 16 + z_ * 2 + core_)

    xr, xl = lax.rem(xi + 1, NX), lax.rem(xi + NX - 1, NX)
    xo = lax.rem(xi + 2, NX)
    zr, zl = lax.rem(z + 1, NZ), lax.rem(z + NZ - 1, NZ)
    zr2, zl2 = lax.rem(z + 2, NZ), lax.rem(z + NZ - 2, NZ)
    oc, oylo, oyhi = 1 - core, 1 - ylo, 1 - yhi

    c_gain = pltpu.make_async_copy(gain, gain_s, ld_s.at[0])
    c_emb = pltpu.make_async_copy(emb, emb_s, ld_s.at[1])
    c_mask = pltpu.make_async_copy(mask, mask_s, ld_s.at[2])
    c_tab = pltpu.make_async_copy(
        tab.at[pl.ds(pl.multiple_of(ctx * ROWS, ROWS), ROWS)], tab_s, ld_s.at[3])
    c_wq = pltpu.make_async_copy(wq, wq_s, ld_s.at[4])
    c_emb.start()
    c_gain.start()

    def xcopies(k):
        cols = pl.ds(pl.multiple_of(k * KB, KB), KB)
        return (
            pltpu.make_async_copy(hid.at[:, cols], x.at[pl.ds(0, ROWS), cols], ld_x.at[k]),
            pltpu.make_async_copy(wk.at[cols], wkv_s.at[cols, pl.ds(0, HD)], ld_k.at[k]),
            pltpu.make_async_copy(wv.at[cols], wkv_s.at[cols, pl.ds(HD, HD)], ld_v.at[k]),
        )

    def start_loads(k, _):
        for c in xcopies(k):
            c.start()
        return 0

    lax.fori_loop(0, NKB, start_loads, 0)
    c_mask.start()
    c_tab.start()
    c_wq.start()

    barrier = pltpu.get_barrier_semaphore()
    partners = [dev(x_=xr), dev(x_=xl), dev(z_=zr2), dev(z_=zl2), dev(z_=zr), dev(z_=zl), dev(core_=oc)]
    for c in (0, 1):
        partners += [dev(ylo_=oylo, core_=c), dev(yhi_=oyhi, core_=c),
                     dev(ylo_=oylo, yhi_=oyhi, core_=c)]
    for p in partners:
        pl.semaphore_signal(barrier, inc=1, device_id=p, device_id_type=MESH)

    my_rows = pl.ds(pl.multiple_of((yhi * 2 + core) * HD, HD), HD)

    def wsrc(half, zz, c):
        return wo.at[:, pl.ds(pl.multiple_of(half * 2048 + zz * 256 + c * HD, HD), HD)]

    def wdst(zz):
        return wd.at[my_rows, pl.ds(pl.multiple_of(zz * HD, HD), HD)]

    def wcopies(zz):
        return (
            pltpu.make_async_copy(wsrc(yhi, zz, core), wdst(zz), ld_w.at[0]),
            pltpu.make_async_remote_copy(
                wsrc(yhi, zz, oc), wdst(zz), w_send.at[0], w_recv.at[0],
                device_id=dev(core_=oc), device_id_type=MESH),
            pltpu.make_async_remote_copy(
                wsrc(oyhi, zz, 0), wdst(zz), w_send.at[1], w_recv.at[1 + core],
                device_id=dev(ylo_=oylo, yhi_=oyhi, core_=0), device_id_type=MESH),
            pltpu.make_async_remote_copy(
                wsrc(oyhi, zz, 1), wdst(zz), w_send.at[2], w_recv.at[1 + core],
                device_id=dev(ylo_=oylo, yhi_=oyhi, core_=1), device_id_type=MESH),
        )

    def start_w(zz, _):
        for c in wcopies(zz):
            c.start()
        return 0

    c_emb.wait()
    c_gain.wait()
    x[pl.ds(ROWS, XROWS - ROWS), :] = jnp.broadcast_to(emb_s[...].reshape(1, D), (XROWS - ROWS, D))
    ss[...] = jnp.zeros_like(ss)
    acc[...] = jnp.zeros_like(acc)

    def kstep(k, _):
        for c in xcopies(k):
            c.wait()
        cols = pl.ds(pl.multiple_of(k * KB, KB), KB)
        xf = x[:, cols].astype(F32)
        sq = xf * xf
        total = sq[:, :128]
        for j in range(1, KB // 128):
            total = total + sq[:, j * 128:(j + 1) * 128]
        ss[...] += total
        xg = (xf * gain_s[:, cols]).astype(BF16)
        x[:, cols] = xg
        acc[...] += jnp.dot(xg, wkv_s[cols, :], preferred_element_type=F32)
        return 0

    lax.fori_loop(0, NKB, kstep, 0)
    c_mask.wait()
    c_tab.wait()
    scale = lax.rsqrt(jnp.sum(ss[...], axis=1, keepdims=True) * (1.0 / D) + 1e-05)
    ss[...] = jnp.broadcast_to(scale, (XROWS, 128))
    flags = (mask_s[...] == 1).astype(F32)
    for i in range(ROWS // 128):
        maskc[pl.ds(i * 128, 128), :] = jnp.transpose(
            jnp.broadcast_to(flags[i:i + 1, :], (128, 128)))

    def chosen(ref, lo):
        u = ref[:, lo:lo + HD] * ss[...]
        return jnp.where(maskc[...] > 0.5, u[ROWS:ROWS + 1, :], u[:ROWS, :])

    lane = lax.broadcasted_iota(jnp.int32, (ROWS, HD), 1)

    def rope(u):
        t = tab_s[...]
        r = pltpu.roll(t, HD // 2, 1)
        c = jnp.where(lane < HD // 2, t, r)
        s = jnp.where(lane < HD // 2, -r, t)
        return u * c + pltpu.roll(u, HD // 2, 1) * s

    me = core * NX + xi
    put = jnp.where(diag, me, 8)
    kv[put, 0] = rope(chosen(acc, 0)).astype(BF16)
    kv[put, 1] = chosen(acc, HD).astype(BF16)

    pl.semaphore_wait(barrier, len(partners))

    partner = dev(ylo_=oylo, core_=oc)
    swap_k = pltpu.make_async_remote_copy(
        kv.at[8, 0], kv.at[ctx, 0], sw_send.at[0], sw_recv.at[0],
        device_id=partner, device_id_type=MESH)
    swap_v = pltpu.make_async_remote_copy(
        kv.at[8, 1], kv.at[ctx, 1], sw_send.at[1], sw_recv.at[1],
        device_id=partner, device_id_type=MESH)
    swap_q = pltpu.make_async_remote_copy(
        qs.at[1], qs.at[0], sw_send.at[2], sw_recv.at[2],
        device_id=partner, device_id_type=MESH)

    OWN, LEFT, RIGHT, OPP = 0, 1, 2, 3
    offs = (xi, xl, xr, xo)
    myset = jnp.where(diag, 0, 1)
    to_r, to_l, to_c = dev(x_=xr), dev(x_=xl), dev(core_=oc)
    HALF = ROWS // 2

    def block(slot, which, half):
        if half is None:
            return kv.at[slot, which]
        return kv.at[slot, which, pl.ds(half * HALF, HALF)]

    def kvcopy(pos, which, half, n, recv, to):
        ref = block(core * NX + offs[pos], which, half)
        return pltpu.make_async_remote_copy(
            ref, ref, kv_send.at[n], recv, device_id=to, device_id_type=MESH)

    own_sends = [
        (kvcopy(OWN, w, None, 3 * w, kv_recv.at[myset, LEFT, w], to_r),
         kvcopy(OWN, w, None, 3 * w + 1, kv_recv.at[myset, RIGHT, w], to_l),
         kvcopy(OWN, w, None, 3 * w + 2, kv_recv.at[myset, OWN, w], to_c)) for w in (0, 1)]
    passes = {}
    for w in (0, 1):
        passes[LEFT, w] = (
            kvcopy(LEFT, w, 0, 6 + w, opp_recv.at[myset, w, 0], to_r),
            kvcopy(LEFT, w, None, 8 + w, kv_recv.at[myset, LEFT, w], to_c))
        passes[RIGHT, w] = (
            kvcopy(RIGHT, w, 1, 10 + w, opp_recv.at[myset, w, 1], to_l),
            kvcopy(RIGHT, w, None, 12 + w, kv_recv.at[myset, RIGHT, w], to_c))
        for h in (0, 1):
            passes[OPP, w, h] = (
                kvcopy(OPP, w, h, 14 + 2 * w + h, opp_recv.at[myset, w, h], to_c),)

    def slot_of(st, pos):
        return (ylo if st == 0 else oylo) * NX + offs[pos]

    def arrived(st, pos, w, h=None):
        ref = block(slot_of(st, pos), w, h)
        sem = kv_recv.at[st, pos, w] if h is None else opp_recv.at[st, w, h]
        pltpu.make_async_copy(ref, ref, sem).wait()

    def pass_on(*key):
        for c in passes[key]:
            c.start()

    @pl.when(diag)
    def _():
        for c in own_sends[0] + own_sends[1]:
            c.start()

    @pl.when(off)
    def _():
        swap_k.start()
        swap_v.start()

    lax.fori_loop(0, NZ, start_w, 0)

    c_wq.wait()
    qacc[...] = jnp.zeros_like(qacc)

    def qstep(k, _):
        cols = pl.ds(pl.multiple_of(k * KQ, KQ), KQ)
        qacc[...] += jnp.dot(x[:, cols], wq_s[cols, :], preferred_element_type=F32)
        return 0

    lax.fori_loop(0, D // KQ, qstep, 0)
    q_factor = math.log2(math.e) / math.sqrt(HD)
    qs[jnp.where(diag, 0, 1)] = (rope(chosen(qacc, 0)) * q_factor).astype(BF16)

    @pl.when(off)
    def _():
        swap_q.start()
        for swap, copies in ((swap_k, own_sends[0]), (swap_v, own_sends[1])):
            swap.wait_recv()
            for c in copies:
                c.start()
        swap_q.wait_recv()
        for w in (0, 1):
            arrived(0, OWN, w)

    ones = jnp.ones((ROWS, HD), BF16)

    def attend_rows(slot, i, first):
        rows = pl.ds(i * QB, QB)
        s = lax.dot_general(qs[0, rows, :], kv[slot, 0], (((1,), (1,)), ((), ())),
                            preferred_element_type=F32)
        top = jnp.broadcast_to(jnp.max(s, axis=1, keepdims=True), (QB, HD))
        if not first:
            old = m_s[rows, :]
            top = jnp.maximum(top, old)
        m_s[rows, :] = top
        p = jnp.exp2(s - jnp.concatenate([top] * (ROWS // HD), axis=1)).astype(BF16)
        v = jnp.concatenate([kv[slot, 1], ones], axis=1)
        add = jnp.dot(p, v, preferred_element_type=F32)
        if first:
            o_s[rows, :] = add
        else:
            alpha = jnp.exp2(old - top)
            o_s[rows, :] = o_s[rows, :] * jnp.concatenate([alpha, alpha], axis=1) + add

    def attend(st, pos):
        for i in range(ROWS // QB):
            attend_rows(slot_of(st, pos), i, st == 0 and pos == OWN)

    def opposite(st, mine):
        for w in (0, 1):
            for h in (0, 1):
                arrived(st, OPP, w, h)
                if mine:
                    pass_on(OPP, w, h)

    attend(0, OWN)

    @pl.when(diag)
    def _():
        for w in (0, 1):
            for pos in (LEFT, RIGHT):
                arrived(0, pos, w)
                pass_on(pos, w)

    @pl.when(off)
    def _():
        for pos in (LEFT, RIGHT):
            arrived(1, pos, 0)
            pass_on(pos, 0)
        for w in (0, 1):
            for pos in (LEFT, RIGHT):
                arrived(0, pos, w)

    attend(0, LEFT)
    attend(0, RIGHT)

    @pl.when(diag)
    def _():
        opposite(0, True)

    @pl.when(off)
    def _():
        for pos in (LEFT, RIGHT):
            arrived(1, pos, 1)
            pass_on(pos, 1)
        opposite(0, False)

    attend(0, OPP)

    @pl.when(diag)
    def _():
        for w in (0, 1):
            arrived(1, OWN, w)

    attend(1, OWN)

    @pl.when(diag)
    def _():
        for w in (0, 1):
            for pos in (LEFT, RIGHT):
                arrived(1, pos, w)

    attend(1, LEFT)
    attend(1, RIGHT)

    @pl.when(off)
    def _():
        opposite(1, True)

    @pl.when(diag)
    def _():
        opposite(1, False)

    hslot = yhi * 2 + ylo
    mcols = pl.ds(pl.multiple_of(hslot * HD, HD), HD)

    def mcopy(r, j):
        rows = pl.ds(r * RB, RB)
        to = (dev(ylo_=core, yhi_=yhi, core_=r % 2), dev(ylo_=core, yhi_=oyhi, core_=r % 2), to_c)[j]
        return pltpu.make_async_remote_copy(
            mixed.at[rows], mbuf.at[rows, mcols], m_send.at[j % 2, r], m_recv.at[hslot, r],
            device_id=to, device_id_type=MESH)

    for i in range(ROWS // QB):
        attend_rows(slot_of(1, OPP), i, False)
        for r in range(i * R * QB // ROWS, (i + 1) * R * QB // ROWS):
            rows = pl.ds(r * RB, RB)
            o = o_s[rows, :]
            mix = (o[:, :HD] / o[:, HD:]).astype(BF16)
            mixed[rows, :] = mix

            @pl.when(off)
            def _():
                mcopy(r, 0).start()

            @pl.when(diag)
            def _():
                mbuf[rows, mcols] = mix
                mcopy(r, 2).start()

            mcopy(r, 1).start()

    own_w = wd.at[my_rows]
    pltpu.make_async_copy(own_w, own_w, ld_w.at[0]).wait()
    for n, slot in ((0, yhi * 2 + oc), (1, oyhi * 2), (2, oyhi * 2 + 1)):
        ref = wd.at[pl.ds(pl.multiple_of(slot * HD, HD), HD)]
        pltpu.make_async_copy(ref, ref, w_recv.at[n]).wait()

    def reaches(d, r):
        return NZ // 2 if (d == 0) == (r < R // 2) else NZ // 2 - 1

    def zcopy(d, r, t):
        to = (zr2, zl2)[d] if t == 4 else (zr, zl)[d]
        return pltpu.make_async_remote_copy(
            sb.at[d, r, t - 1], rb.at[d, r, t - 1], z_send.at[d, r, t - 1], z_recv.at[d, r, t - 1],
            device_id=dev(z_=to), device_id_type=MESH)

    def piece(r, dest):
        return part[pl.ds(r * RB, RB), pl.ds(pl.multiple_of(dest * HD, HD), HD)]

    def mpass(h, r):
        ref = mbuf.at[pl.ds(r * RB, RB), pl.ds(h * HD, HD)]
        return pltpu.make_async_remote_copy(
            ref, ref, p_send.at[h, r], m_recv.at[h, r], device_id=to_c, device_id_type=MESH)

    def partial(r):
        rows = pl.ds(r * RB, RB)
        for h in range(4):
            def wait_slot():
                ref = mbuf.at[rows, pl.ds(h * HD, HD)]
                pltpu.make_async_copy(ref, ref, m_recv.at[h, r]).wait()

            def pass_on():
                mpass(h, r).start()

            pl.when(jnp.logical_or(off, hslot != h))(wait_slot)
            pl.when(jnp.logical_and(core == r % 2, hslot != h))(pass_on)
        part[rows, :] = jnp.dot(mbuf[rows, :], wd[...], preferred_element_type=F32)

    def zsend(r, t):
        for d in (0, 1):
            if t > reaches(d, r):
                continue
            val = piece(r, lax.rem(z + (t if d == 0 else NZ - t), NZ))
            for u in ((), (2,), (3, 4), (), ())[t]:
                if u <= reaches(d, r):
                    zcopy(d, r, u).wait_recv()
                    val = val + rb[d, r, u - 1].astype(F32)
            sb[d, r, t - 1] = val.astype(BF16)
            zcopy(d, r, t).start()

    for r in range(R):
        partial(r)
        zsend(r, 4)
        zsend(r, 3)
    for t in (2, 1):
        for r in range(R):
            zsend(r, t)
    for r in range(R):
        val = piece(r, z)
        for d in (0, 1):
            zcopy(d, r, 1).wait_recv()
            val = val + rb[d, r, 0].astype(F32)
        out[pl.ds(r * RB, RB), :] = val.astype(BF16)

    for n, c in ((0, oc), (1, 0), (2, 1)):
        pltpu.make_async_copy(own_w, own_w, w_send.at[n]).wait()

    @pl.when(off)
    def _():
        for c in (swap_k, swap_v, swap_q):
            c.wait_send()

    for c in own_sends[0] + own_sends[1]:
        c.wait_send()
    for copies in passes.values():
        for c in copies:
            c.wait_send()
    for r in range(R):
        mcopy(r, 0).wait_send()
        mcopy(r, 1).wait_send()
        for h in range(4):
            pl.when(jnp.logical_and(core == r % 2, hslot != h))(mpass(h, r).wait_send)
        for d in (0, 1):
            for t in range(1, reaches(d, r) + 1):
                zcopy(d, r, t).wait_send()


def on_device(hidden, mask_flags, mask_embed, norm_gain, w_query, w_key, w_value, w_out):
    any_spec = pl.BlockSpec(memory_space=pl.ANY)
    dma = pltpu.SemaphoreType.DMA
    return pl.pallas_call(
        kernel,
        out_shape=jax.ShapeDtypeStruct((ROWS, HD), BF16),
        in_specs=[any_spec] * 9,
        out_specs=pl.BlockSpec(memory_space=pltpu.VMEM),
        scratch_shapes=[
            pltpu.VMEM((XROWS, D), BF16),
            pltpu.VMEM((D, 2 * HD), BF16),
            pltpu.VMEM((D, HD), BF16),
            pltpu.VMEM((D,), BF16),
            pltpu.VMEM((1, D), F32),
            pltpu.VMEM((ROWS // 128, 128), jnp.int32),
            pltpu.VMEM((ROWS, HD), F32),
            pltpu.VMEM((ROWS, 128), F32),
            pltpu.VMEM((XROWS, 128), F32),
            pltpu.VMEM((XROWS, 2 * HD), F32),
            pltpu.VMEM((XROWS, HD), F32),
            pltpu.VMEM((9, 2, ROWS, HD), BF16),
            pltpu.VMEM((2, ROWS, HD), BF16),
            pltpu.VMEM((ROWS, HD), F32),
            pltpu.VMEM((ROWS, 2 * HD), F32),
            pltpu.VMEM((ROWS, HD), BF16),
            pltpu.VMEM((ROWS, 4 * HD), BF16),
            pltpu.VMEM((4 * HD, NZ * HD), BF16),
            pltpu.VMEM((ROWS, NZ * HD), F32),
            pltpu.VMEM((2, R, NZ // 2, RB, HD), BF16),
            pltpu.VMEM((2, R, NZ // 2, RB, HD), BF16),
            dma((NKB,)), dma((NKB,)), dma((NKB,)), dma((5,)), dma((1,)),
            dma((3,)), dma((3,)), dma((3,)), dma((3,)),
            dma((18,)), dma((2, 3, 2)), dma((2, 2, 2)), dma((2, R)), dma((4, R)), dma((4, R)),
            dma((2, R, NZ // 2)), dma((2, R, NZ // 2)),
        ],
        compiler_params=pltpu.CompilerParams(
            collective_id=0, has_side_effects=True, vmem_limit_bytes=62 * 1024 * 1024),
    )(hidden, mask_flags.reshape(ROWS // 128, 128), mask_embed,
      norm_gain.reshape(1, D), w_query, w_key, w_value, w_out, jnp.asarray(rope_table()))


def solution(mesh):
    in_specs = (
        P("ctx", None),
        P("ctx"),
        P(),
        P(),
        P(None, "tp"),
        P(None, "tp"),
        P(None, "tp"),
        P("tp", None),
    )
    return jax.shard_map(
        on_device, mesh=mesh, in_specs=in_specs, out_specs=P("ctx", "tp"), check_vma=False
    )
```

```python
import math

import numpy as np
import jax
import jax.numpy as jnp
from jax import lax
from jax.sharding import PartitionSpec as P
from jax.experimental import pallas as pl
from jax.experimental.pallas import tpu as pltpu

D = 4096
HD = 128
SEQ = 4096
ROWS = 512
XROWS = 528
KB = 1024
NKB = D // KB
KQ = 512
R = 4
RB = ROWS // R
QB = 256
NZ = 8
NX = 4
MESH = pl.DeviceIdType.MESH
F32 = jnp.float32
BF16 = jnp.bfloat16


def rope_table():
    freqs = 500000.0 ** (-2.0 * np.arange(HD // 2) / HD)
    angles = np.arange(SEQ)[:, None] * freqs[None, :]
    return np.concatenate([np.cos(angles), np.sin(angles)], axis=1).astype(np.float32)


def kernel(hid, mask, emb, gain, wq, wk, wv, wo, tab, out,
           x, wkv_s, wq_s, emb_s, gain_s, mask_s, tab_s, maskc, ss, acc, qacc,
           kv, qs, m_s, o_s, pay, rx, acol, mbuf, wd, part, rb, sb,
           ld_x, ld_k, ld_v, ld_s, ld_w, w_send, w_recv, q_sem,
           kv_send, kv_recv, opp_recv, m_send, m_recv, p_send, p_recv, z_send, z_recv):
    ctx = lax.axis_index("ctx")
    tp = lax.axis_index("tp")
    xi, ylo = lax.rem(ctx, NX), lax.div(ctx, NX)
    yhi, z, core = lax.div(tp, 16), lax.rem(lax.div(tp, 2), NZ), lax.rem(tp, 2)

    def dev(x_=xi, ylo_=ylo, yhi_=yhi, z_=z, core_=core):
        return (ylo_ * NX + x_, yhi_ * 16 + z_ * 2 + core_)

    xr, xl = lax.rem(xi + 1, NX), lax.rem(xi + NX - 1, NX)
    xo = lax.rem(xi + 2, NX)
    zr, zl = lax.rem(z + 1, NZ), lax.rem(z + NZ - 1, NZ)
    zr2, zl2 = lax.rem(z + 2, NZ), lax.rem(z + NZ - 2, NZ)
    oc, oylo, oyhi = 1 - core, 1 - ylo, 1 - yhi

    c_gain = pltpu.make_async_copy(gain, gain_s, ld_s.at[0])
    c_emb = pltpu.make_async_copy(emb, emb_s, ld_s.at[1])
    c_mask = pltpu.make_async_copy(mask, mask_s, ld_s.at[2])
    c_tab = pltpu.make_async_copy(
        tab.at[pl.ds(pl.multiple_of(ctx * ROWS, ROWS), ROWS)], tab_s, ld_s.at[3])
    c_wq = pltpu.make_async_copy(wq, wq_s, ld_s.at[4])
    c_emb.start()
    c_gain.start()

    def xcopies(k):
        cols = pl.ds(pl.multiple_of(k * KB, KB), KB)
        return (
            pltpu.make_async_copy(hid.at[:, cols], x.at[pl.ds(0, ROWS), cols], ld_x.at[k]),
            pltpu.make_async_copy(wk.at[cols], wkv_s.at[cols, pl.ds(0, HD)], ld_k.at[k]),
            pltpu.make_async_copy(wv.at[cols], wkv_s.at[cols, pl.ds(HD, HD)], ld_v.at[k]),
        )

    def start_loads(k, _):
        for c in xcopies(k):
            c.start()
        return 0

    lax.fori_loop(0, NKB, start_loads, 0)
    c_mask.start()
    c_tab.start()
    c_wq.start()

    barrier = pltpu.get_barrier_semaphore()
    partners = [dev(x_=xr), dev(x_=xl), dev(z_=zr2), dev(z_=zl2), dev(z_=zr), dev(z_=zl), dev(core_=oc)]
    for c in (0, 1):
        partners += [dev(ylo_=oylo, core_=c), dev(yhi_=oyhi, core_=c),
                     dev(ylo_=oylo, yhi_=oyhi, core_=c)]
    for p in partners:
        pl.semaphore_signal(barrier, inc=1, device_id=p, device_id_type=MESH)

    my_rows = pl.ds(pl.multiple_of((yhi * 2 + core) * HD, HD), HD)

    def wsrc(half, zz, c):
        return wo.at[:, pl.ds(pl.multiple_of(half * 2048 + zz * 256 + c * HD, HD), HD)]

    def wdst(zz):
        return wd.at[zz, my_rows]

    def wcopies(zz):
        return (
            pltpu.make_async_copy(wsrc(yhi, zz, core), wdst(zz), ld_w.at[0]),
            pltpu.make_async_remote_copy(
                wsrc(yhi, zz, oc), wdst(zz), w_send.at[0], w_recv.at[0],
                device_id=dev(core_=oc), device_id_type=MESH),
            pltpu.make_async_remote_copy(
                wsrc(oyhi, zz, 0), wdst(zz), w_send.at[1], w_recv.at[1 + core],
                device_id=dev(ylo_=oylo, yhi_=oyhi, core_=0), device_id_type=MESH),
            pltpu.make_async_remote_copy(
                wsrc(oyhi, zz, 1), wdst(zz), w_send.at[2], w_recv.at[1 + core],
                device_id=dev(ylo_=oylo, yhi_=oyhi, core_=1), device_id_type=MESH),
        )

    def start_w(zz, _):
        for c in wcopies(zz):
            c.start()
        return 0

    c_emb.wait()
    c_gain.wait()
    x[pl.ds(ROWS, XROWS - ROWS), :] = jnp.broadcast_to(emb_s[...].reshape(1, D), (XROWS - ROWS, D))
    ss[...] = jnp.zeros_like(ss)
    acc[...] = jnp.zeros_like(acc)

    def kstep(k, _):
        for c in xcopies(k):
            c.wait()
        cols = pl.ds(pl.multiple_of(k * KB, KB), KB)
        xf = x[:, cols].astype(F32)
        sq = xf * xf
        total = sq[:, :128]
        for j in range(1, KB // 128):
            total = total + sq[:, j * 128:(j + 1) * 128]
        ss[...] += total
        xg = (xf * gain_s[:, cols]).astype(BF16)
        x[:, cols] = xg
        acc[...] += jnp.dot(xg, wkv_s[cols, :], preferred_element_type=F32)
        return 0

    lax.fori_loop(0, NKB, kstep, 0)
    c_mask.wait()
    c_tab.wait()
    scale = lax.rsqrt(jnp.sum(ss[...], axis=1, keepdims=True) * (1.0 / D) + 1e-05)
    ss[...] = jnp.broadcast_to(scale, (XROWS, 128))
    flags = (mask_s[...] == 1).astype(F32)
    for i in range(ROWS // 128):
        maskc[pl.ds(i * 128, 128), :] = jnp.transpose(
            jnp.broadcast_to(flags[i:i + 1, :], (128, 128)))

    def chosen(ref, lo):
        u = ref[:, lo:lo + HD] * ss[...]
        return jnp.where(maskc[...] > 0.5, u[ROWS:ROWS + 1, :], u[:ROWS, :])

    lane = lax.broadcasted_iota(jnp.int32, (ROWS, HD), 1)

    def rope(u):
        t = tab_s[...]
        r = pltpu.roll(t, HD // 2, 1)
        c = jnp.where(lane < HD // 2, t, r)
        s = jnp.where(lane < HD // 2, -r, t)
        return u * c + pltpu.roll(u, HD // 2, 1) * s

    kv[xi, 0] = rope(chosen(acc, 0)).astype(BF16)
    kv[xi, 1] = chosen(acc, HD).astype(BF16)

    pl.semaphore_wait(barrier, len(partners))

    OWN, LEFT, RIGHT, OPP = 0, 1, 2, 3
    slots = (xi, xl, xr, xo)
    to_r, to_l, to_c = dev(x_=xr), dev(x_=xl), dev(core_=oc)
    HALF = ROWS // 2

    def block(pos, w, half):
        if half is None:
            return kv.at[slots[pos], w]
        return kv.at[slots[pos], w, pl.ds(half * HALF, HALF)]

    def kvcopy(pos, w, half, n, recv, to):
        ref = block(pos, w, half)
        return pltpu.make_async_remote_copy(
            ref, ref, kv_send.at[n], recv, device_id=to, device_id_type=MESH)

    own_sends = []
    passes = {}
    for w in (0, 1):
        own_sends += [kvcopy(OWN, w, None, 2 * w, kv_recv.at[0, w], to_r),
                      kvcopy(OWN, w, None, 2 * w + 1, kv_recv.at[1, w], to_l)]
        passes[LEFT, w] = kvcopy(LEFT, w, 0, 4 + w, opp_recv.at[w, 0], to_r)
        passes[RIGHT, w] = kvcopy(RIGHT, w, 1, 6 + w, opp_recv.at[w, 1], to_l)

    def arrived(pos, w, h=None):
        ref = block(pos, w, h)
        sem = kv_recv.at[pos - LEFT, w] if h is None else opp_recv.at[w, h]
        pltpu.make_async_copy(ref, ref, sem).wait()

    for c in own_sends:
        c.start()

    lax.fori_loop(0, NZ, start_w, 0)

    c_wq.wait()
    qacc[...] = jnp.zeros_like(qacc)

    def qstep(k, _):
        cols = pl.ds(pl.multiple_of(k * KQ, KQ), KQ)
        qacc[...] += jnp.dot(x[:, cols], wq_s[cols, :], preferred_element_type=F32)
        return 0

    lax.fori_loop(0, D // KQ, qstep, 0)
    q_factor = math.log2(math.e) / math.sqrt(HD)
    qs[0] = (rope(chosen(qacc, 0)) * q_factor).astype(BF16)

    q_send = pltpu.make_async_remote_copy(
        qs.at[0], qs.at[1], q_sem.at[0], q_sem.at[1], device_id=dev(ylo_=oylo), device_id_type=MESH)
    q_send.start()

    ones = jnp.ones((ROWS, HD), BF16)

    def attend_rows(qset, pos, i):
        rows = pl.ds(i * QB, QB)
        slot = slots[pos]
        s = lax.dot_general(qs[qset, rows, :], kv[slot, 0], (((1,), (1,)), ((), ())),
                            preferred_element_type=F32)
        top = jnp.broadcast_to(jnp.max(s, axis=1, keepdims=True), (QB, HD))
        if pos != OWN:
            old = m_s[qset, rows, :]
            top = jnp.maximum(top, old)
        m_s[qset, rows, :] = top
        p = jnp.exp2(s - jnp.concatenate([top] * (ROWS // HD), axis=1)).astype(BF16)
        v = jnp.concatenate([kv[slot, 1], ones], axis=1)
        add = jnp.dot(p, v, preferred_element_type=F32)
        if pos == OWN:
            o_s[qset, rows, :] = add
        else:
            alpha = jnp.exp2(old - top)
            o_s[qset, rows, :] = o_s[qset, rows, :] * jnp.concatenate([alpha, alpha], axis=1) + add

    def attend(qset, pos):
        for i in range(ROWS // QB):
            attend_rows(qset, pos, i)

    attend(0, OWN)
    for w in (0, 1):
        for pos in (LEFT, RIGHT):
            arrived(pos, w)
            passes[pos, w].start()
    attend(0, LEFT)
    attend(0, RIGHT)
    q_send.wait_recv()
    attend(1, OWN)
    attend(1, LEFT)
    attend(1, RIGHT)
    for w in (0, 1):
        for h in (0, 1):
            arrived(OPP, w, h)

    myh = yhi * 2 + core
    HB = RB // 2
    piece_row = lax.broadcasted_iota(jnp.int32, (16, 128), 0)

    def mcopy(r, n, c):
        qset = (1, 1, 0)[n]
        to = (dev(ylo_=oylo, core_=c), dev(ylo_=oylo, yhi_=oyhi, core_=c), dev(yhi_=oyhi, core_=c))[n]
        return pltpu.make_async_remote_copy(
            pay.at[qset, r, c], rx.at[qset, myh, r], m_send.at[r, 2 * n + c],
            m_recv.at[qset, myh, r], device_id=to, device_id_type=MESH)

    def mbeside(r):
        return pltpu.make_async_remote_copy(
            pay.at[0, r, oc], rx.at[0, myh, r], m_send.at[r, 6],
            m_recv.at[0, myh, r], device_id=to_c, device_id_type=MESH)

    def pack(qset, r):
        rows = pl.ds(r * RB, RB)
        o = o_s[qset, rows, :]
        mix = (o[:, :HD] / o[:, HD:]).astype(BF16)
        lse = jnp.transpose(m_s[qset, rows, :] + jnp.log2(o[:, HD:]))[:16, :]
        hi = lse.astype(BF16).astype(F32)
        mid = (lse - hi).astype(BF16).astype(F32)
        low = lse - hi - mid
        stat = jnp.where(piece_row == 0, hi, jnp.where(piece_row == 1, mid, low)).astype(BF16)
        for c in (0, 1):
            pay[qset, r, c, pl.ds(0, HB), :] = mix[c * HB:(c + 1) * HB]
            pay[qset, r, c, pl.ds(HB, 16), :] = stat

    for i in range(ROWS // QB):
        attend_rows(1, OPP, i)
        attend_rows(0, OPP, i)
        for r in range(i * R * QB // ROWS, (i + 1) * R * QB // ROWS):
            pack(1, r)
            pack(0, r)
            for n in range(3):
                for c in (0, 1):
                    mcopy(r, n, c).start()
            mbeside(r).start()
            rx[0, myh, r] = pay[0, r, core]

    own_w = wd.at[:, my_rows]
    pltpu.make_async_copy(own_w, own_w, ld_w.at[0]).wait()
    for n, slot in ((0, yhi * 2 + oc), (1, oyhi * 2), (2, oyhi * 2 + 1)):
        ref = wd.at[:, pl.ds(pl.multiple_of(slot * HD, HD), HD)]
        pltpu.make_async_copy(ref, ref, w_recv.at[n]).wait()

    def reaches(d, r):
        return NZ // 2 if (d == 0) == (r < R // 2) else NZ // 2 - 1

    def zcopy(d, r, t):
        to = (zr2, zl2)[d] if t == 4 else (zr, zl)[d]
        return pltpu.make_async_remote_copy(
            sb.at[d, r, t - 1], rb.at[d, r, t - 1], z_send.at[d, r, t - 1], z_recv.at[d, r, t - 1],
            device_id=dev(z_=to), device_id_type=MESH)

    def piece(r, dest):
        return part[dest, pl.ds(r * RB, RB)]

    def mhalf(r, c):
        return mbuf.at[pl.ds(pl.multiple_of(r * RB + c * HB, HB), HB)]

    def mpass(r):
        return pltpu.make_async_remote_copy(
            mhalf(r, core), mhalf(r, core), p_send.at[r], p_recv.at[r],
            device_id=to_c, device_id_type=MESH)

    def take(r):
        for k in range(4):
            h = lax.rem(myh + k, 4)
            for n in (0, 1) if k else (1,):
                ref = rx.at[n, h, r]
                pltpu.make_async_copy(ref, ref, m_recv.at[n, h, r]).wait()
        for h in range(4):
            logs = []
            for n in (0, 1):
                t = rx[n, h, r, pl.ds(HB, 16), :].astype(F32)
                logs.append(t[0:1] + t[1:2] + t[2:3])
            share = 1.0 / (1.0 + jnp.exp2(logs[1] - logs[0]))
            acol[h] = jnp.transpose(jnp.broadcast_to(share, (128, 128)))
        rows = pl.ds(pl.multiple_of(r * RB + core * HB, HB), HB)
        for h in range(4):
            a = acol[h, pl.ds(pl.multiple_of(core * HB, HB), HB), :]
            u = rx[0, h, r, pl.ds(0, HB), :].astype(F32)
            v = rx[1, h, r, pl.ds(0, HB), :].astype(F32)
            mbuf[rows, pl.ds(h * HD, HD)] = (u * a + v * (1.0 - a)).astype(BF16)
        mpass(r).start()

    def taken(r):
        pltpu.make_async_copy(mhalf(r, oc), mhalf(r, oc), p_recv.at[r]).wait()

    def partial(rows, a, b):
        a, b = lax.rem(z + NZ + a, NZ), lax.rem(z + NZ + b, NZ)
        both = jnp.dot(mbuf[rows, :], jnp.concatenate([wd[a], wd[b]], axis=1),
                       preferred_element_type=F32)
        part[a, rows] = both[:, :HD]
        part[b, rows] = both[:, HD:]

    def zsend(r, t):
        for d in (0, 1):
            if t > reaches(d, r):
                continue
            val = piece(r, lax.rem(z + (t if d == 0 else NZ - t), NZ))
            for u in ((), (2,), (3, 4), (), ())[t]:
                if u <= reaches(d, r):
                    zcopy(d, r, u).wait_recv()
                    val = val + rb[d, r, u - 1].astype(F32)
            sb[d, r, t - 1] = val.astype(BF16)
            zcopy(d, r, t).start()

    take(0)
    for r in range(R):
        if r + 1 < R:
            take(r + 1)
        taken(r)
        rows = pl.ds(r * RB, RB)
        partial(rows, 4, 3)
        partial(rows, -3, -2)
        zsend(r, 4)
        zsend(r, 3)
    partial(pl.ds(0, ROWS), 2, 1)
    partial(pl.ds(0, ROWS), -1, 0)
    for t in (2, 1):
        for r in range(R):
            zsend(r, t)
    for r in range(R):
        val = piece(r, z)
        for d in (0, 1):
            zcopy(d, r, 1).wait_recv()
            val = val + rb[d, r, 0].astype(F32)
        out[pl.ds(r * RB, RB), :] = val.astype(BF16)

    for n, c in ((0, oc), (1, 0), (2, 1)):
        pltpu.make_async_copy(own_w, own_w, w_send.at[n]).wait()

    q_send.wait_send()
    for c in own_sends + list(passes.values()):
        c.wait_send()
    for r in range(R):
        for n in range(3):
            for c in (0, 1):
                mcopy(r, n, c).wait_send()
        mbeside(r).wait_send()
        mpass(r).wait_send()
        for d in (0, 1):
            for t in range(1, reaches(d, r) + 1):
                zcopy(d, r, t).wait_send()


def on_device(hidden, mask_flags, mask_embed, norm_gain, w_query, w_key, w_value, w_out):
    any_spec = pl.BlockSpec(memory_space=pl.ANY)
    dma = pltpu.SemaphoreType.DMA
    return pl.pallas_call(
        kernel,
        out_shape=jax.ShapeDtypeStruct((ROWS, HD), BF16),
        in_specs=[any_spec] * 9,
        out_specs=pl.BlockSpec(memory_space=pltpu.VMEM),
        scratch_shapes=[
            pltpu.VMEM((XROWS, D), BF16),
            pltpu.VMEM((D, 2 * HD), BF16),
            pltpu.VMEM((D, HD), BF16),
            pltpu.VMEM((D,), BF16),
            pltpu.VMEM((1, D), F32),
            pltpu.VMEM((ROWS // 128, 128), jnp.int32),
            pltpu.VMEM((ROWS, HD), F32),
            pltpu.VMEM((ROWS, 128), F32),
            pltpu.VMEM((XROWS, 128), F32),
            pltpu.VMEM((XROWS, 2 * HD), F32),
            pltpu.VMEM((XROWS, HD), F32),
            pltpu.VMEM((NX, 2, ROWS, HD), BF16),
            pltpu.VMEM((2, ROWS, HD), BF16),
            pltpu.VMEM((2, ROWS, HD), F32),
            pltpu.VMEM((2, ROWS, 2 * HD), F32),
            pltpu.VMEM((2, R, 2, RB // 2 + 16, HD), BF16),
            pltpu.VMEM((2, 4, R, RB // 2 + 16, HD), BF16),
            pltpu.VMEM((4, 128, 128), F32),
            pltpu.VMEM((ROWS, 4 * HD), BF16),
            pltpu.VMEM((NZ, 4 * HD, HD), BF16),
            pltpu.VMEM((NZ, ROWS, HD), F32),
            pltpu.VMEM((2, R, NZ // 2, RB, HD), BF16),
            pltpu.VMEM((2, R, NZ // 2, RB, HD), BF16),
            dma((NKB,)), dma((NKB,)), dma((NKB,)), dma((5,)), dma((1,)),
            dma((3,)), dma((3,)), dma((2,)),
            dma((8,)), dma((2, 2)), dma((2, 2)), dma((R, 7)), dma((2, 4, R)), dma((R,)), dma((R,)),
            dma((2, R, NZ // 2)), dma((2, R, NZ // 2)),
        ],
        compiler_params=pltpu.CompilerParams(
            collective_id=0, has_side_effects=True, vmem_limit_bytes=62 * 1024 * 1024),
    )(hidden, mask_flags.reshape(ROWS // 128, 128), mask_embed,
      norm_gain.reshape(1, D), w_query, w_key, w_value, w_out, jnp.asarray(rope_table()))


def solution(mesh):
    in_specs = (
        P("ctx", None),
        P("ctx"),
        P(),
        P(),
        P(None, "tp"),
        P(None, "tp"),
        P(None, "tp"),
        P("tp", None),
    )
    return jax.shard_map(
        on_device, mesh=mesh, in_specs=in_specs, out_specs=P("ctx", "tp"), check_vma=False
    )
```

```python
import math

import numpy as np
import jax
import jax.numpy as jnp
from jax import lax
from jax.sharding import PartitionSpec as P
from jax.experimental import pallas as pl
from jax.experimental.pallas import tpu as pltpu

D = 4096
HD = 128
SEQ = 4096
ROWS = 512
XROWS = 528
KB = 1024
NKB = D // KB
KQ = 512
R = 4
RB = ROWS // R
QB = 256
NZ = 8
NX = 4
MESH = pl.DeviceIdType.MESH
F32 = jnp.float32
BF16 = jnp.bfloat16


def rope_table():
    freqs = 500000.0 ** (-2.0 * np.arange(HD // 2) / HD)
    angles = np.arange(SEQ)[:, None] * freqs[None, :]
    return np.concatenate([np.cos(angles), np.sin(angles)], axis=1).astype(np.float32)


def kernel(hid, mask, emb, gain, wq, wk, wv, wo, tab, out,
           x, wkv_s, wq_s, emb_s, gain_s, mask_s, tab_s, maskc, ss, acc, qacc,
           kv, qs, m_s, o_s, pay, rx, mbuf, wd, part, rb, sb,
           ld_x, ld_k, ld_v, ld_s, ld_w, w_send, w_recv, q_sem,
           kv_send, kv_recv, opp_recv, m_send, m_recv, p_send, p_recv, z_send, z_recv):
    ctx = lax.axis_index("ctx")
    tp = lax.axis_index("tp")
    xi, ylo = lax.rem(ctx, NX), lax.div(ctx, NX)
    yhi, z, core = lax.div(tp, 16), lax.rem(lax.div(tp, 2), NZ), lax.rem(tp, 2)

    def dev(x_=xi, ylo_=ylo, yhi_=yhi, z_=z, core_=core):
        return (ylo_ * NX + x_, yhi_ * 16 + z_ * 2 + core_)

    xr, xl = lax.rem(xi + 1, NX), lax.rem(xi + NX - 1, NX)
    xo = lax.rem(xi + 2, NX)
    zr, zl = lax.rem(z + 1, NZ), lax.rem(z + NZ - 1, NZ)
    zr2, zl2 = lax.rem(z + 2, NZ), lax.rem(z + NZ - 2, NZ)
    oc, oylo, oyhi = 1 - core, 1 - ylo, 1 - yhi

    c_gain = pltpu.make_async_copy(gain, gain_s, ld_s.at[0])
    c_emb = pltpu.make_async_copy(emb, emb_s, ld_s.at[1])
    c_mask = pltpu.make_async_copy(mask, mask_s, ld_s.at[2])
    c_tab = pltpu.make_async_copy(
        tab.at[pl.ds(pl.multiple_of(ctx * ROWS, ROWS), ROWS)], tab_s, ld_s.at[3])
    c_wq = pltpu.make_async_copy(wq, wq_s, ld_s.at[4])
    c_emb.start()
    c_gain.start()

    def xcopies(k):
        cols = pl.ds(pl.multiple_of(k * KB, KB), KB)
        return (
            pltpu.make_async_copy(hid.at[:, cols], x.at[pl.ds(0, ROWS), cols], ld_x.at[k]),
            pltpu.make_async_copy(wk.at[cols], wkv_s.at[cols, pl.ds(0, HD)], ld_k.at[k]),
            pltpu.make_async_copy(wv.at[cols], wkv_s.at[cols, pl.ds(HD, HD)], ld_v.at[k]),
        )

    def start_loads(k, _):
        for c in xcopies(k):
            c.start()
        return 0

    lax.fori_loop(0, NKB, start_loads, 0)
    c_mask.start()
    c_tab.start()
    c_wq.start()

    barrier = pltpu.get_barrier_semaphore()
    partners = [dev(x_=xr), dev(x_=xl), dev(z_=zr2), dev(z_=zl2), dev(z_=zr), dev(z_=zl), dev(core_=oc)]
    for c in (0, 1):
        partners += [dev(ylo_=oylo, core_=c), dev(yhi_=oyhi, core_=c),
                     dev(ylo_=oylo, yhi_=oyhi, core_=c)]
    for p in partners:
        pl.semaphore_signal(barrier, inc=1, device_id=p, device_id_type=MESH)

    my_rows = pl.ds(pl.multiple_of((yhi * 2 + core) * HD, HD), HD)

    def wsrc(half, zz, c):
        return wo.at[:, pl.ds(pl.multiple_of(half * 2048 + zz * 256 + c * HD, HD), HD)]

    def wdst(zz):
        return wd.at[zz, my_rows]

    def wcopies(zz):
        return (
            pltpu.make_async_copy(wsrc(yhi, zz, core), wdst(zz), ld_w.at[0]),
            pltpu.make_async_remote_copy(
                wsrc(yhi, zz, oc), wdst(zz), w_send.at[0], w_recv.at[0],
                device_id=dev(core_=oc), device_id_type=MESH),
            pltpu.make_async_remote_copy(
                wsrc(oyhi, zz, 0), wdst(zz), w_send.at[1], w_recv.at[1 + core],
                device_id=dev(ylo_=oylo, yhi_=oyhi, core_=0), device_id_type=MESH),
            pltpu.make_async_remote_copy(
                wsrc(oyhi, zz, 1), wdst(zz), w_send.at[2], w_recv.at[1 + core],
                device_id=dev(ylo_=oylo, yhi_=oyhi, core_=1), device_id_type=MESH),
        )

    def start_w(zz, _):
        for c in wcopies(zz):
            c.start()
        return 0

    c_emb.wait()
    c_gain.wait()
    x[pl.ds(ROWS, XROWS - ROWS), :] = jnp.broadcast_to(emb_s[...].reshape(1, D), (XROWS - ROWS, D))
    ss[...] = jnp.zeros_like(ss)
    acc[...] = jnp.zeros_like(acc)

    def kstep(k, _):
        for c in xcopies(k):
            c.wait()
        cols = pl.ds(pl.multiple_of(k * KB, KB), KB)
        xf = x[:, cols].astype(F32)
        sq = xf * xf
        total = sq[:, :128]
        for j in range(1, KB // 128):
            total = total + sq[:, j * 128:(j + 1) * 128]
        ss[...] += total
        xg = (xf * gain_s[:, cols]).astype(BF16)
        x[:, cols] = xg
        acc[...] += jnp.dot(xg, wkv_s[cols, :], preferred_element_type=F32)
        return 0

    lax.fori_loop(0, NKB, kstep, 0)
    c_mask.wait()
    c_tab.wait()
    scale = lax.rsqrt(jnp.sum(ss[...], axis=1, keepdims=True) * (1.0 / D) + 1e-05)
    ss[...] = jnp.broadcast_to(scale, (XROWS, 128))
    flags = (mask_s[...] == 1).astype(F32)
    for i in range(ROWS // 128):
        maskc[pl.ds(i * 128, 128), :] = jnp.transpose(
            jnp.broadcast_to(flags[i:i + 1, :], (128, 128)))

    def chosen(ref, lo):
        u = ref[:, lo:lo + HD] * ss[...]
        return jnp.where(maskc[...] > 0.5, u[ROWS:ROWS + 1, :], u[:ROWS, :])

    lane = lax.broadcasted_iota(jnp.int32, (ROWS, HD), 1)

    def rope(u):
        t = tab_s[...]
        r = pltpu.roll(t, HD // 2, 1)
        c = jnp.where(lane < HD // 2, t, r)
        s = jnp.where(lane < HD // 2, -r, t)
        return u * c + pltpu.roll(u, HD // 2, 1) * s

    kv[xi, 0] = rope(chosen(acc, 0)).astype(BF16)
    kv[xi, 1] = chosen(acc, HD).astype(BF16)

    pl.semaphore_wait(barrier, len(partners))

    OWN, LEFT, RIGHT, OPP = 0, 1, 2, 3
    slots = (xi, xl, xr, xo)
    to_r, to_l, to_c = dev(x_=xr), dev(x_=xl), dev(core_=oc)
    HALF = ROWS // 2

    def block(pos, w, half):
        if half is None:
            return kv.at[slots[pos], w]
        return kv.at[slots[pos], w, pl.ds(half * HALF, HALF)]

    def kvcopy(pos, w, half, n, recv, to):
        ref = block(pos, w, half)
        return pltpu.make_async_remote_copy(
            ref, ref, kv_send.at[n], recv, device_id=to, device_id_type=MESH)

    own_sends = []
    passes = {}
    for w in (0, 1):
        own_sends += [kvcopy(OWN, w, None, 2 * w, kv_recv.at[0, w], to_r),
                      kvcopy(OWN, w, None, 2 * w + 1, kv_recv.at[1, w], to_l)]
        passes[LEFT, w] = kvcopy(LEFT, w, 0, 4 + w, opp_recv.at[w, 0], to_r)
        passes[RIGHT, w] = kvcopy(RIGHT, w, 1, 6 + w, opp_recv.at[w, 1], to_l)

    def arrived(pos, w, h=None):
        ref = block(pos, w, h)
        sem = kv_recv.at[pos - LEFT, w] if h is None else opp_recv.at[w, h]
        pltpu.make_async_copy(ref, ref, sem).wait()

    for c in own_sends:
        c.start()

    lax.fori_loop(0, NZ, start_w, 0)

    c_wq.wait()
    qacc[...] = jnp.zeros_like(qacc)

    def qstep(k, _):
        cols = pl.ds(pl.multiple_of(k * KQ, KQ), KQ)
        qacc[...] += jnp.dot(x[:, cols], wq_s[cols, :], preferred_element_type=F32)
        return 0

    lax.fori_loop(0, D // KQ, qstep, 0)
    q_factor = math.log2(math.e) / math.sqrt(HD)
    qs[0] = (rope(chosen(qacc, 0)) * q_factor).astype(BF16)

    q_send = pltpu.make_async_remote_copy(
        qs.at[0], qs.at[1], q_sem.at[0], q_sem.at[1], device_id=dev(ylo_=oylo), device_id_type=MESH)
    q_send.start()

    ones = jnp.ones((ROWS, HD), BF16)

    def attend_rows(qset, pos, i, n=QB):
        rows = pl.ds(i * n, n)
        slot = slots[pos]
        s = lax.dot_general(qs[qset, rows, :], kv[slot, 0], (((1,), (1,)), ((), ())),
                            preferred_element_type=F32)
        top = jnp.broadcast_to(jnp.max(s, axis=1, keepdims=True), (n, HD))
        if pos != OWN:
            old = m_s[qset, rows, :]
            top = jnp.maximum(top, old)
        m_s[qset, rows, :] = top
        p = jnp.exp2(s - jnp.concatenate([top] * (ROWS // HD), axis=1)).astype(BF16)
        v = jnp.concatenate([kv[slot, 1], ones], axis=1)
        add = jnp.dot(p, v, preferred_element_type=F32)
        if pos == OWN:
            o_s[qset, rows, :] = add
        else:
            alpha = jnp.exp2(old - top)
            o_s[qset, rows, :] = o_s[qset, rows, :] * jnp.concatenate([alpha, alpha], axis=1) + add

    def attend(qset, pos):
        for i in range(ROWS // QB):
            attend_rows(qset, pos, i)

    attend(0, OWN)
    for w in (0, 1):
        for pos in (LEFT, RIGHT):
            arrived(pos, w)
            passes[pos, w].start()
    attend(0, LEFT)
    attend(0, RIGHT)
    q_send.wait_recv()
    attend(1, OWN)
    attend(1, LEFT)
    attend(1, RIGHT)
    for w in (0, 1):
        for h in (0, 1):
            arrived(OPP, w, h)

    myh = yhi * 2 + core
    piece_row = lax.broadcasted_iota(jnp.int32, (16, 128), 0)

    def mcopy(r, n):
        qset = (1, 1, 0, 0)[n]
        c = r % 2
        to = (dev(ylo_=oylo, core_=c), dev(ylo_=oylo, yhi_=oyhi, core_=c), dev(yhi_=oyhi, core_=c), to_c)[n]
        return pltpu.make_async_remote_copy(
            pay.at[qset, r], rx.at[qset, myh, r], m_send.at[r, n],
            m_recv.at[qset, myh, r], device_id=to, device_id_type=MESH)

    def pack(qset, r):
        rows = pl.ds(r * RB, RB)
        o = o_s[qset, rows, :]
        lse = jnp.transpose(m_s[qset, rows, :] + jnp.log2(o[:, HD:]))[:16, :]
        hi = lse.astype(BF16).astype(F32)
        mid = (lse - hi).astype(BF16).astype(F32)
        low = lse - hi - mid
        stat = jnp.where(piece_row == 0, hi, jnp.where(piece_row == 1, mid, low))
        pay[qset, r, pl.ds(0, RB), :] = (o[:, :HD] / o[:, HD:]).astype(BF16)
        pay[qset, r, pl.ds(RB, 16), :] = stat.astype(BF16)

    for r in range(R):
        attend_rows(1, OPP, r, RB)
        pack(1, r)
        mcopy(r, 0).start()
        mcopy(r, 1).start()
        attend_rows(0, OPP, r, RB)
        pack(0, r)
        mcopy(r, 2).start()

        @pl.when(core == r % 2)
        def _():
            rx[0, myh, r] = pay[0, r]

        @pl.when(core != r % 2)
        def _():
            mcopy(r, 3).start()

    own_w = wd.at[:, my_rows]
    pltpu.make_async_copy(own_w, own_w, ld_w.at[0]).wait()
    for n, slot in ((0, yhi * 2 + oc), (1, oyhi * 2), (2, oyhi * 2 + 1)):
        ref = wd.at[:, pl.ds(pl.multiple_of(slot * HD, HD), HD)]
        pltpu.make_async_copy(ref, ref, w_recv.at[n]).wait()

    def reaches(d, r):
        return NZ // 2 if (d == 0) == (r % 2 == 0) else NZ // 2 - 1

    def zcopy(d, r, t):
        to = (zr2, zl2)[d] if t == 4 else (zr, zl)[d]
        return pltpu.make_async_remote_copy(
            sb.at[d, r, t - 1], rb.at[d, r, t - 1], z_send.at[d, r, t - 1], z_recv.at[d, r, t - 1],
            device_id=dev(z_=to), device_id_type=MESH)

    def piece(r, dest):
        return part[dest, pl.ds(r * RB, RB)]

    def mpass(r):
        ref = mbuf.at[pl.ds(r * RB, RB)]
        return pltpu.make_async_remote_copy(
            ref, ref, p_send.at[r], p_recv.at[r], device_id=to_c, device_id_type=MESH)

    def take(r):
        for k in range(4):
            h = lax.rem(myh + k, 4)
            for n in (0, 1) if k else (1,):
                ref = rx.at[n, h, r]
                pltpu.make_async_copy(ref, ref, m_recv.at[n, h, r]).wait()
        for h in range(4):
            logs = []
            for n in (0, 1):
                t = rx[n, h, r, pl.ds(RB, 16), :].astype(F32)
                logs.append(t[0:1] + t[1:2] + t[2:3])
            share = 1.0 / (1.0 + jnp.exp2(logs[1] - logs[0]))
            a = jnp.transpose(jnp.broadcast_to(share, (RB, HD)))
            u = rx[0, h, r, pl.ds(0, RB), :].astype(F32)
            v = rx[1, h, r, pl.ds(0, RB), :].astype(F32)
            mbuf[pl.ds(r * RB, RB), pl.ds(h * HD, HD)] = (u * a + v * (1.0 - a)).astype(BF16)
        mpass(r).start()

    def partial(rows, a, b):
        a, b = lax.rem(z + NZ + a, NZ), lax.rem(z + NZ + b, NZ)
        both = jnp.dot(mbuf[rows, :], jnp.concatenate([wd[a], wd[b]], axis=1),
                       preferred_element_type=F32)
        part[a, rows] = both[:, :HD]
        part[b, rows] = both[:, HD:]

    def zsend(r, t):
        for d in (0, 1):
            if t > reaches(d, r):
                continue
            val = piece(r, lax.rem(z + (t if d == 0 else NZ - t), NZ))
            for u in ((), (2,), (3, 4), (), ())[t]:
                if u <= reaches(d, r):
                    zcopy(d, r, u).wait_recv()
                    val = val + rb[d, r, u - 1].astype(F32)
            sb[d, r, t - 1] = val.astype(BF16)
            zcopy(d, r, t).start()

    for r in range(R):
        @pl.when(core == r % 2)
        def _():
            take(r)

        pl.when(core != r % 2)(mpass(r).wait_recv)
        rows = pl.ds(r * RB, RB)
        partial(rows, 4, 3)
        partial(rows, -3, -2)
        zsend(r, 4)
        zsend(r, 3)
    partial(pl.ds(0, ROWS), 2, 1)
    partial(pl.ds(0, ROWS), -1, 0)
    for t in (2, 1):
        for r in range(R):
            zsend(r, t)
    for r in range(R):
        val = piece(r, z)
        for d in (0, 1):
            zcopy(d, r, 1).wait_recv()
            val = val + rb[d, r, 0].astype(F32)
        out[pl.ds(r * RB, RB), :] = val.astype(BF16)

    for n, c in ((0, oc), (1, 0), (2, 1)):
        pltpu.make_async_copy(own_w, own_w, w_send.at[n]).wait()

    q_send.wait_send()
    for c in own_sends + list(passes.values()):
        c.wait_send()
    for r in range(R):
        for n in range(3):
            mcopy(r, n).wait_send()
        pl.when(core != r % 2)(mcopy(r, 3).wait_send)
        pl.when(core == r % 2)(mpass(r).wait_send)
        for d in (0, 1):
            for t in range(1, reaches(d, r) + 1):
                zcopy(d, r, t).wait_send()


def on_device(hidden, mask_flags, mask_embed, norm_gain, w_query, w_key, w_value, w_out):
    any_spec = pl.BlockSpec(memory_space=pl.ANY)
    dma = pltpu.SemaphoreType.DMA
    return pl.pallas_call(
        kernel,
        out_shape=jax.ShapeDtypeStruct((ROWS, HD), BF16),
        in_specs=[any_spec] * 9,
        out_specs=pl.BlockSpec(memory_space=pltpu.VMEM),
        scratch_shapes=[
            pltpu.VMEM((XROWS, D), BF16),
            pltpu.VMEM((D, 2 * HD), BF16),
            pltpu.VMEM((D, HD), BF16),
            pltpu.VMEM((D,), BF16),
            pltpu.VMEM((1, D), F32),
            pltpu.VMEM((ROWS // 128, 128), jnp.int32),
            pltpu.VMEM((ROWS, HD), F32),
            pltpu.VMEM((ROWS, 128), F32),
            pltpu.VMEM((XROWS, 128), F32),
            pltpu.VMEM((XROWS, 2 * HD), F32),
            pltpu.VMEM((XROWS, HD), F32),
            pltpu.VMEM((NX, 2, ROWS, HD), BF16),
            pltpu.VMEM((2, ROWS, HD), BF16),
            pltpu.VMEM((2, ROWS, HD), F32),
            pltpu.VMEM((2, ROWS, 2 * HD), F32),
            pltpu.VMEM((2, R, RB + 16, HD), BF16),
            pltpu.VMEM((2, 4, R, RB + 16, HD), BF16),
            pltpu.VMEM((ROWS, 4 * HD), BF16),
            pltpu.VMEM((NZ, 4 * HD, HD), BF16),
            pltpu.VMEM((NZ, ROWS, HD), F32),
            pltpu.VMEM((2, R, NZ // 2, RB, HD), BF16),
            pltpu.VMEM((2, R, NZ // 2, RB, HD), BF16),
            dma((NKB,)), dma((NKB,)), dma((NKB,)), dma((5,)), dma((1,)),
            dma((3,)), dma((3,)), dma((2,)),
            dma((8,)), dma((2, 2)), dma((2, 2)), dma((R, 4)), dma((2, 4, R)), dma((R,)), dma((R,)),
            dma((2, R, NZ // 2)), dma((2, R, NZ // 2)),
        ],
        compiler_params=pltpu.CompilerParams(
            collective_id=0, has_side_effects=True, vmem_limit_bytes=62 * 1024 * 1024),
    )(hidden, mask_flags.reshape(ROWS // 128, 128), mask_embed,
      norm_gain.reshape(1, D), w_query, w_key, w_value, w_out, jnp.asarray(rope_table()))


def solution(mesh):
    in_specs = (
        P("ctx", None),
        P("ctx"),
        P(),
        P(),
        P(None, "tp"),
        P(None, "tp"),
        P(None, "tp"),
        P("tp", None),
    )
    return jax.shard_map(
        on_device, mesh=mesh, in_specs=in_specs, out_specs=P("ctx", "tp"), check_vma=False
    )
```

```python
import math

import numpy as np
import jax
import jax.numpy as jnp
from jax import lax
from jax.sharding import PartitionSpec as P
from jax.experimental import pallas as pl
from jax.experimental.pallas import tpu as pltpu

D = 4096
HD = 128
SEQ = 4096
ROWS = 512
XROWS = 528
KB = 1024
NKB = D // KB
KQ = 512
R = 4
RB = ROWS // R
QB = 256
NZ = 8
NX = 4
MESH = pl.DeviceIdType.MESH
F32 = jnp.float32
BF16 = jnp.bfloat16


def rope_table():
    freqs = 500000.0 ** (-2.0 * np.arange(HD // 2) / HD)
    angles = np.arange(SEQ)[:, None] * freqs[None, :]
    return np.concatenate([np.cos(angles), np.sin(angles)], axis=1).astype(np.float32)


def kernel(hid, mask, emb, gain, wq, wk, wv, wo, tab, out,
           x, wkv_s, wq_s, emb_s, gain_s, mask_s, tab_s, maskc, ss, acc, qacc,
           kv, qs, m_s, o_s, pay, rx, mbuf, wd, part, rb, sb,
           ld_x, ld_k, ld_v, ld_s, ld_w, w_send, w_recv, q_sem,
           kv_send, kv_recv, opp_recv, m_send, m_recv, p_send, p_recv, z_send, z_recv):
    ctx = lax.axis_index("ctx")
    tp = lax.axis_index("tp")
    xi, ylo = lax.rem(ctx, NX), lax.div(ctx, NX)
    yhi, z, core = lax.div(tp, 16), lax.rem(lax.div(tp, 2), NZ), lax.rem(tp, 2)

    def dev(x_=xi, ylo_=ylo, yhi_=yhi, z_=z, core_=core):
        return (ylo_ * NX + x_, yhi_ * 16 + z_ * 2 + core_)

    xr, xl = lax.rem(xi + 1, NX), lax.rem(xi + NX - 1, NX)
    xo = lax.rem(xi + 2, NX)
    zr, zl = lax.rem(z + 1, NZ), lax.rem(z + NZ - 1, NZ)
    zr2, zl2 = lax.rem(z + 2, NZ), lax.rem(z + NZ - 2, NZ)
    oc, oylo, oyhi = 1 - core, 1 - ylo, 1 - yhi

    c_gain = pltpu.make_async_copy(gain, gain_s, ld_s.at[0])
    c_emb = pltpu.make_async_copy(emb, emb_s, ld_s.at[1])
    c_mask = pltpu.make_async_copy(mask, mask_s, ld_s.at[2])
    c_tab = pltpu.make_async_copy(
        tab.at[pl.ds(pl.multiple_of(ctx * ROWS, ROWS), ROWS)], tab_s, ld_s.at[3])
    c_wq = pltpu.make_async_copy(wq, wq_s, ld_s.at[4])
    c_emb.start()
    c_gain.start()

    def xcopies(k):
        cols = pl.ds(pl.multiple_of(k * KB, KB), KB)
        return (
            pltpu.make_async_copy(hid.at[:, cols], x.at[pl.ds(0, ROWS), cols], ld_x.at[k]),
            pltpu.make_async_copy(wk.at[cols], wkv_s.at[cols, pl.ds(0, HD)], ld_k.at[k]),
            pltpu.make_async_copy(wv.at[cols], wkv_s.at[cols, pl.ds(HD, HD)], ld_v.at[k]),
        )

    def start_loads(k, _):
        for c in xcopies(k):
            c.start()
        return 0

    lax.fori_loop(0, NKB, start_loads, 0)
    c_mask.start()
    c_tab.start()
    c_wq.start()

    barrier = pltpu.get_barrier_semaphore()
    partners = [dev(x_=xr), dev(x_=xl), dev(z_=zr2), dev(z_=zl2), dev(z_=zr), dev(z_=zl), dev(core_=oc)]
    for c in (0, 1):
        partners += [dev(ylo_=oylo, core_=c), dev(yhi_=oyhi, core_=c),
                     dev(ylo_=oylo, yhi_=oyhi, core_=c)]
    for p in partners:
        pl.semaphore_signal(barrier, inc=1, device_id=p, device_id_type=MESH)

    my_rows = pl.ds(pl.multiple_of((yhi * 2 + core) * HD, HD), HD)

    def wsrc(half, j, c):
        zz = lax.rem(z + 3 + j, NZ)
        return wo.at[:, pl.ds(pl.multiple_of(half * 2048 + zz * 256 + c * HD, HD), HD)]

    def wcopies(zz):
        g = zz // 4
        return (
            pltpu.make_async_copy(wsrc(yhi, zz, core), wd.at[zz, my_rows], ld_w.at[g]),
            pltpu.make_async_remote_copy(
                wsrc(yhi, zz, oc), wd.at[zz, my_rows], w_send.at[0], w_recv.at[g, 0],
                device_id=dev(core_=oc), device_id_type=MESH),
            pltpu.make_async_remote_copy(
                wsrc(oyhi, zz, 0), wd.at[zz, my_rows], w_send.at[1], w_recv.at[g, 1 + core],
                device_id=dev(ylo_=oylo, yhi_=oyhi, core_=0), device_id_type=MESH),
            pltpu.make_async_remote_copy(
                wsrc(oyhi, zz, 1), wd.at[zz, my_rows], w_send.at[2], w_recv.at[g, 1 + core],
                device_id=dev(ylo_=oylo, yhi_=oyhi, core_=1), device_id_type=MESH),
        )

    c_emb.wait()
    c_gain.wait()
    x[pl.ds(ROWS, XROWS - ROWS), :] = jnp.broadcast_to(emb_s[...].reshape(1, D), (XROWS - ROWS, D))
    ss[...] = jnp.zeros_like(ss)
    acc[...] = jnp.zeros_like(acc)

    def kstep(k, _):
        for c in xcopies(k):
            c.wait()
        cols = pl.ds(pl.multiple_of(k * KB, KB), KB)
        xf = x[:, cols].astype(F32)
        sq = xf * xf
        total = sq[:, :128]
        for j in range(1, KB // 128):
            total = total + sq[:, j * 128:(j + 1) * 128]
        ss[...] += total
        xg = (xf * gain_s[:, cols]).astype(BF16)
        x[:, cols] = xg
        acc[...] += jnp.dot(xg, wkv_s[cols, :], preferred_element_type=F32)
        return 0

    lax.fori_loop(0, NKB, kstep, 0)
    c_mask.wait()
    c_tab.wait()
    scale = lax.rsqrt(jnp.sum(ss[...], axis=1, keepdims=True) * (1.0 / D) + 1e-05)
    ss[...] = jnp.broadcast_to(scale, (XROWS, 128))
    flags = (mask_s[...] == 1).astype(F32)
    for i in range(ROWS // 128):
        maskc[pl.ds(i * 128, 128), :] = jnp.transpose(
            jnp.broadcast_to(flags[i:i + 1, :], (128, 128)))

    def chosen(ref, lo):
        u = ref[:, lo:lo + HD] * ss[...]
        return jnp.where(maskc[...] > 0.5, u[ROWS:ROWS + 1, :], u[:ROWS, :])

    lane = lax.broadcasted_iota(jnp.int32, (ROWS, HD), 1)

    def rope(u):
        t = tab_s[...]
        r = pltpu.roll(t, HD // 2, 1)
        c = jnp.where(lane < HD // 2, t, r)
        s = jnp.where(lane < HD // 2, -r, t)
        return u * c + pltpu.roll(u, HD // 2, 1) * s

    kv[xi, 0] = rope(chosen(acc, 0)).astype(BF16)
    kv[xi, 1] = chosen(acc, HD).astype(BF16)

    pl.semaphore_wait(barrier, len(partners))

    OWN, LEFT, RIGHT, OPP = 0, 1, 2, 3
    slots = (xi, xl, xr, xo)
    to_r, to_l, to_c = dev(x_=xr), dev(x_=xl), dev(core_=oc)
    HALF = ROWS // 2

    def block(pos, w, half):
        if half is None:
            return kv.at[slots[pos], w]
        return kv.at[slots[pos], w, pl.ds(half * HALF, HALF)]

    def kvcopy(pos, w, half, n, recv, to):
        ref = block(pos, w, half)
        return pltpu.make_async_remote_copy(
            ref, ref, kv_send.at[n], recv, device_id=to, device_id_type=MESH)

    own_sends = []
    passes = {}
    for w in (0, 1):
        own_sends += [kvcopy(OWN, w, None, 2 * w, kv_recv.at[0, w], to_r),
                      kvcopy(OWN, w, None, 2 * w + 1, kv_recv.at[1, w], to_l)]
        passes[LEFT, w] = kvcopy(LEFT, w, 0, 4 + w, opp_recv.at[w, 0], to_r)
        passes[RIGHT, w] = kvcopy(RIGHT, w, 1, 6 + w, opp_recv.at[w, 1], to_l)

    def arrived(pos, w, h=None):
        ref = block(pos, w, h)
        sem = kv_recv.at[pos - LEFT, w] if h is None else opp_recv.at[w, h]
        pltpu.make_async_copy(ref, ref, sem).wait()

    for c in own_sends:
        c.start()

    for j in range(NZ):
        for c in wcopies(j):
            c.start()

    c_wq.wait()
    qacc[...] = jnp.zeros_like(qacc)

    def qstep(k, _):
        cols = pl.ds(pl.multiple_of(k * KQ, KQ), KQ)
        qacc[...] += jnp.dot(x[:, cols], wq_s[cols, :], preferred_element_type=F32)
        return 0

    lax.fori_loop(0, D // KQ, qstep, 0)
    q_factor = math.log2(math.e) / math.sqrt(HD)
    qs[0] = (rope(chosen(qacc, 0)) * q_factor).astype(BF16)

    q_send = pltpu.make_async_remote_copy(
        qs.at[0], qs.at[1], q_sem.at[0], q_sem.at[1], device_id=dev(ylo_=oylo), device_id_type=MESH)
    q_send.start()

    ones = jnp.ones((ROWS, HD), BF16)

    def attend_rows(qset, pos, i, n=QB):
        rows = pl.ds(i * n, n)
        slot = slots[pos]
        s = lax.dot_general(qs[qset, rows, :], kv[slot, 0], (((1,), (1,)), ((), ())),
                            preferred_element_type=F32)
        top = jnp.broadcast_to(jnp.max(s, axis=1, keepdims=True), (n, HD))
        if pos != OWN:
            old = m_s[qset, rows, :]
            top = jnp.maximum(top, old)
        m_s[qset, rows, :] = top
        p = jnp.exp2(s - jnp.concatenate([top] * (ROWS // HD), axis=1)).astype(BF16)
        v = jnp.concatenate([kv[slot, 1], ones], axis=1)
        add = jnp.dot(p, v, preferred_element_type=F32)
        if pos == OWN:
            o_s[qset, rows, :] = add
        else:
            alpha = jnp.exp2(old - top)
            o_s[qset, rows, :] = o_s[qset, rows, :] * jnp.concatenate([alpha, alpha], axis=1) + add

    def attend(qset, pos):
        for i in range(ROWS // QB):
            attend_rows(qset, pos, i)

    attend(0, OWN)
    for w in (0, 1):
        for pos in (LEFT, RIGHT):
            arrived(pos, w)
            passes[pos, w].start()
    attend(0, LEFT)
    attend(0, RIGHT)
    q_send.wait_recv()
    attend(1, OWN)
    attend(1, LEFT)
    attend(1, RIGHT)
    for w in (0, 1):
        for h in (0, 1):
            arrived(OPP, w, h)

    myh = yhi * 2 + core
    piece_row = lax.broadcasted_iota(jnp.int32, (16, 128), 0)

    def mcopy(r, n):
        qset = (1, 1, 0, 0)[n]
        c = r % 2
        to = (dev(ylo_=oylo, core_=c), dev(ylo_=oylo, yhi_=oyhi, core_=c), dev(yhi_=oyhi, core_=c), to_c)[n]
        return pltpu.make_async_remote_copy(
            pay.at[qset, r], rx.at[qset, myh, r], m_send.at[r, n],
            m_recv.at[qset, myh, r], device_id=to, device_id_type=MESH)

    def pack(qset, r):
        rows = pl.ds(r * RB, RB)
        o = o_s[qset, rows, :]
        lse = jnp.transpose(m_s[qset, rows, :] + jnp.log2(o[:, HD:]))[:16, :]
        hi = lse.astype(BF16).astype(F32)
        mid = (lse - hi).astype(BF16).astype(F32)
        low = lse - hi - mid
        stat = jnp.where(piece_row == 0, hi, jnp.where(piece_row == 1, mid, low))
        pay[qset, r, pl.ds(0, RB), :] = (o[:, :HD] / o[:, HD:]).astype(BF16)
        pay[qset, r, pl.ds(RB, 16), :] = stat.astype(BF16)

    for r in range(R):
        attend_rows(1, OPP, r, RB)
        pack(1, r)
        mcopy(r, 0).start()
        mcopy(r, 1).start()
        attend_rows(0, OPP, r, RB)
        pack(0, r)
        mcopy(r, 2).start()

        @pl.when(core == r % 2)
        def _():
            rx[0, myh, r] = pay[0, r]

        @pl.when(core != r % 2)
        def _():
            mcopy(r, 3).start()

    own_w = wd.at[:, my_rows]

    def w_here(g):
        for n, slot in ((None, yhi * 2 + core), (0, yhi * 2 + oc), (1, oyhi * 2), (2, oyhi * 2 + 1)):
            ref = wd.at[pl.ds(4 * g, 4), pl.ds(pl.multiple_of(slot * HD, HD), HD)]
            sem = ld_w.at[g] if n is None else w_recv.at[g, n]
            pltpu.make_async_copy(ref, ref, sem).wait()

    w_here(0)

    def reaches(d, r):
        return NZ // 2 if (d == 0) == (r % 2 == 0) else NZ // 2 - 1

    def zcopy(d, r, t):
        to = (zr2, zl2)[d] if t == 4 else (zr, zl)[d]
        return pltpu.make_async_remote_copy(
            sb.at[d, r, t - 1], rb.at[d, r, t - 1], z_send.at[d, r, t - 1], z_recv.at[d, r, t - 1],
            device_id=dev(z_=to), device_id_type=MESH)

    def piece(r, ahead):
        return part[(ahead - 3) % NZ, pl.ds(r * RB, RB)]

    def mpass(r):
        ref = mbuf.at[pl.ds(r * RB, RB)]
        return pltpu.make_async_remote_copy(
            ref, ref, p_send.at[r], p_recv.at[r], device_id=to_c, device_id_type=MESH)

    def take(r):
        for k in range(4):
            h = lax.rem(myh + k, 4)
            for n in (0, 1) if k else (1,):
                ref = rx.at[n, h, r]
                pltpu.make_async_copy(ref, ref, m_recv.at[n, h, r]).wait()
        for h in range(4):
            logs = []
            for n in (0, 1):
                t = rx[n, h, r, pl.ds(RB, 16), :].astype(F32)
                logs.append(t[0:1] + t[1:2] + t[2:3])
            share = 1.0 / (1.0 + jnp.exp2(logs[1] - logs[0]))
            a = jnp.transpose(jnp.broadcast_to(share, (RB, HD)))
            u = rx[0, h, r, pl.ds(0, RB), :].astype(F32)
            v = rx[1, h, r, pl.ds(0, RB), :].astype(F32)
            mbuf[pl.ds(r * RB, RB), pl.ds(h * HD, HD)] = (u * a + v * (1.0 - a)).astype(BF16)
        mpass(r).start()

    def partial(rows, a, b):
        a, b = (a - 3) % NZ, (b - 3) % NZ
        both = jnp.dot(mbuf[rows, :], jnp.concatenate([wd[a], wd[b]], axis=1),
                       preferred_element_type=F32)
        part[a, rows] = both[:, :HD]
        part[b, rows] = both[:, HD:]

    def zsend(r, t):
        for d in (0, 1):
            if t > reaches(d, r):
                continue
            val = piece(r, t if d == 0 else -t)
            for u in ((), (2,), (3, 4), (), ())[t]:
                if u <= reaches(d, r):
                    zcopy(d, r, u).wait_recv()
                    val = val + rb[d, r, u - 1].astype(F32)
            sb[d, r, t - 1] = val.astype(BF16)
            zcopy(d, r, t).start()

    for r in range(R):
        if r == 0:
            @pl.when(core == 0)
            def _():
                take(0)

        @pl.when(core != r % 2)
        def _():
            if r + 1 < R:
                take(r + 1)
            mpass(r).wait_recv()
        rows = pl.ds(r * RB, RB)
        partial(rows, 4, 3)
        partial(rows, -3, -2)
        zsend(r, 4)
        zsend(r, 3)
    w_here(1)
    partial(pl.ds(0, ROWS), 2, 1)
    partial(pl.ds(0, ROWS), -1, 0)
    for t in (2, 1):
        for r in range(R):
            zsend(r, t)
    for r in range(R):
        val = piece(r, 0)
        for d in (0, 1):
            zcopy(d, r, 1).wait_recv()
            val = val + rb[d, r, 0].astype(F32)
        out[pl.ds(r * RB, RB), :] = val.astype(BF16)

    for n, c in ((0, oc), (1, 0), (2, 1)):
        pltpu.make_async_copy(own_w, own_w, w_send.at[n]).wait()

    q_send.wait_send()
    for c in own_sends + list(passes.values()):
        c.wait_send()
    for r in range(R):
        for n in range(3):
            mcopy(r, n).wait_send()
        pl.when(core != r % 2)(mcopy(r, 3).wait_send)
        pl.when(core == r % 2)(mpass(r).wait_send)
        for d in (0, 1):
            for t in range(1, reaches(d, r) + 1):
                zcopy(d, r, t).wait_send()


def on_device(hidden, mask_flags, mask_embed, norm_gain, w_query, w_key, w_value, w_out):
    any_spec = pl.BlockSpec(memory_space=pl.ANY)
    dma = pltpu.SemaphoreType.DMA
    return pl.pallas_call(
        kernel,
        out_shape=jax.ShapeDtypeStruct((ROWS, HD), BF16),
        in_specs=[any_spec] * 9,
        out_specs=pl.BlockSpec(memory_space=pltpu.VMEM),
        scratch_shapes=[
            pltpu.VMEM((XROWS, D), BF16),
            pltpu.VMEM((D, 2 * HD), BF16),
            pltpu.VMEM((D, HD), BF16),
            pltpu.VMEM((D,), BF16),
            pltpu.VMEM((1, D), F32),
            pltpu.VMEM((ROWS // 128, 128), jnp.int32),
            pltpu.VMEM((ROWS, HD), F32),
            pltpu.VMEM((ROWS, 128), F32),
            pltpu.VMEM((XROWS, 128), F32),
            pltpu.VMEM((XROWS, 2 * HD), F32),
            pltpu.VMEM((XROWS, HD), F32),
            pltpu.VMEM((NX, 2, ROWS, HD), BF16),
            pltpu.VMEM((2, ROWS, HD), BF16),
            pltpu.VMEM((2, ROWS, HD), F32),
            pltpu.VMEM((2, ROWS, 2 * HD), F32),
            pltpu.VMEM((2, R, RB + 16, HD), BF16),
            pltpu.VMEM((2, 4, R, RB + 16, HD), BF16),
            pltpu.VMEM((ROWS, 4 * HD), BF16),
            pltpu.VMEM((NZ, 4 * HD, HD), BF16),
            pltpu.VMEM((NZ, ROWS, HD), F32),
            pltpu.VMEM((2, R, NZ // 2, RB, HD), BF16),
            pltpu.VMEM((2, R, NZ // 2, RB, HD), BF16),
            dma((NKB,)), dma((NKB,)), dma((NKB,)), dma((5,)), dma((2,)),
            dma((3,)), dma((2, 3)), dma((2,)),
            dma((8,)), dma((2, 2)), dma((2, 2)), dma((R, 4)), dma((2, 4, R)), dma((R,)), dma((R,)),
            dma((2, R, NZ // 2)), dma((2, R, NZ // 2)),
        ],
        compiler_params=pltpu.CompilerParams(
            collective_id=0, has_side_effects=True, vmem_limit_bytes=62 * 1024 * 1024),
    )(hidden, mask_flags.reshape(ROWS // 128, 128), mask_embed,
      norm_gain.reshape(1, D), w_query, w_key, w_value, w_out, jnp.asarray(rope_table()))


def solution(mesh):
    in_specs = (
        P("ctx", None),
        P("ctx"),
        P(),
        P(),
        P(None, "tp"),
        P(None, "tp"),
        P(None, "tp"),
        P("tp", None),
    )
    return jax.shard_map(
        on_device, mesh=mesh, in_specs=in_specs, out_specs=P("ctx", "tp"), check_vma=False
    )
```
